128 devices in a mesh: jpair: 8 (over z, y_lo), row: 16 (over x, y_hi, core).
Axes of the slice: x: 4, y: 4 (y_hi: 2, y_lo: 2; y = y_hi * 2 + y_lo), z: 4, core: 2. Of those that a mesh axis runs over, the one named last changes fastest.
Arguments:
- s_real: bfloat16 [8, 3072, 3072], P('jpair', 'row'), may hold values from -0.67578125 to 0.67578125
- s_imag: bfloat16 [8, 3072, 3072], P('jpair', 'row'), may hold values from -0.67578125 to 0.67578125
- chan_l: int32 [8, 3072], P('jpair'), may hold values from 0 to 31
- counts: int32 [8], P('jpair'), may hold values from 2304 to 2688, as said below
- jlevel: int32 [8], P('jpair'), may hold values from 0 to 47
- allowed: int32 [32, 32], replicated, may hold values 0 or 1
- recoup: float32 [32, 32], replicated, may hold values from 0.3 to 3
Outputs:
- relax: float32 [8, 3072, 3072], P('jpair', 'row')
The draws below stay inside these ranges and needn't reach their ends.
Inputs may be any that keep to these rules, and one draw needn't show every extreme that they name: `counts`: every block has at least three quarters of its channels open and at most 2688; some block has exactly 2688 open.
All inputs are finite; a program needn't handle non-finite values.
Results may differ from the reference program's by a relative error of at most 0.0003.
Values may be sent and summed in bfloat16 or wider, within the bound.
A program may use at most 128 MiB of HBM per device.

```python
import math
import jax
import jax.numpy as jnp
from jax import lax

C = 3072
LMAX = 32
JBLOCKS = 8
N_ROW = 16


def draw_counts(key, part):
    key = jax.random.fold_in(key, 5)
    first_key, second_key = jax.random.split(key)
    values = jax.random.randint(first_key, (JBLOCKS,), 3 * C // 4, 7 * C // 8 + 1)
    chosen = jax.random.randint(second_key, (), 0, JBLOCKS)
    return jnp.where(jnp.arange(JBLOCKS) == chosen, 7 * C // 8, values).astype(jnp.int32)


def place_ends(result, key, least, high):
    shape = result.shape
    place = [jax.random.randint(jax.random.fold_in(key, axis), (), 0, shape[axis]) for axis in range(len(shape))]
    result = result.at[tuple(place)].set(least)
    longest = shape.index(max(shape))
    place[longest] = (place[longest] + 1) % shape[longest]
    return result.at[tuple(place)].set(high)


def block_levels(key, shape, cuts, smallest, largest):
    level = 1.0
    for axis_at, shards_of in cuts:
        heights = jax.random.uniform(jax.random.fold_in(jax.random.fold_in(key, 6), axis_at), (shards_of,), jnp.float32, smallest / len(cuts), largest / len(cuts))
        level = level * jnp.repeat(jnp.exp(heights), shape[axis_at] // shards_of).reshape((-1,) + (1,) * (len(shape) - 1 - axis_at))
    return level


def bell_draw(stream_key, extent, width, bound, cuts=(), held_as=jnp.bfloat16):
    values = jax.random.normal(stream_key, extent, jnp.float32) * width
    if len(cuts) > 0:
        values = block_levels(stream_key, extent, cuts, -0.22, 0.18) * values
    return jnp.clip(values, min=-bound, max=bound).astype(held_as)


def setup_inputs(seed: int = 0) -> dict:
    splits = jax.random.split(jax.random.key(seed), 8)
    s_real = bell_draw(splits[0], (JBLOCKS, C, C), (1.0 / (2 * C) ** 0.25), 0.67578125, ((0, 8), (1, 16)))
    s_imag = bell_draw(splits[1], (JBLOCKS, C, C), (1.0 / (2 * C) ** 0.25), 0.67578125, ((0, 8), (1, 16)))
    chan_l = place_ends(jax.random.randint(splits[2], (JBLOCKS, C), 0, LMAX), jax.random.fold_in(splits[2], 1), 0, LMAX - 1).astype(jnp.int32)
    counts = draw_counts(jax.random.fold_in(splits[7], 71), 0)
    jlevel = place_ends(jax.random.randint(splits[4], (JBLOCKS,), 0, 48), jax.random.fold_in(splits[4], 1), 0, 47).astype(jnp.int32)
    allowed = place_ends((jax.random.randint(splits[5], (LMAX, LMAX), 0, 2) < 1).astype(jnp.int32), jax.random.fold_in(splits[5], 1), 0, 1)
    recoup = jnp.clip(jnp.exp(jax.random.uniform(splits[6], (LMAX, LMAX), jnp.float32, math.log(0.3), math.log(3.0))), 0.3, 3.0)
    return {"s_real": s_real, "s_imag": s_imag, "chan_l": chan_l, "counts": counts, "jlevel": jlevel, "allowed": allowed, "recoup": recoup}


def closed_block(s_real, s_imag, counts, block_id):
    channel_ids = jnp.arange(C)
    live = channel_ids < counts[block_id]
    both_live = live[:, None] & live[None, :]
    zeros_bf = jnp.zeros((C, C), jnp.bfloat16)
    return jnp.where(both_live, s_real[block_id], zeros_bf), jnp.where(both_live, s_imag[block_id], zeros_bf)


def reference(s_real, s_imag, chan_l, counts, jlevel, allowed, recoup):
    slab_rows = C // N_ROW
    weight_table = recoup * allowed.astype(jnp.float32)
    results = []
    for pair_no in range(JBLOCKS // 2):
        upper_id = 2 * pair_no
        lower_id = 2 * pair_no + 1
        up_re, up_im = closed_block(s_real, s_imag, counts, upper_id)
        low_re, low_im = closed_block(s_real, s_imag, counts, lower_id)

        def add_slab(totals, block_no):
            row_start = (block_no * slab_rows).astype(jnp.int32)
            ur = lax.dynamic_slice_in_dim(up_re, row_start, slab_rows, 0)
            ui = lax.dynamic_slice_in_dim(up_im, row_start, slab_rows, 0)
            wr = lax.dynamic_slice_in_dim(low_re, row_start, slab_rows, 0)
            wi = lax.dynamic_slice_in_dim(low_im, row_start, slab_rows, 0)
            left_side = jnp.concatenate([ur, ui], 0)
            real_part = jnp.dot(left_side.T, jnp.concatenate([wr, wi], 0), preferred_element_type=jnp.float32)
            imag_part = jnp.dot(left_side.T, jnp.concatenate([wi, -wr], 0), preferred_element_type=jnp.float32)
            return (totals[0] + real_part, totals[1] + imag_part), None

        start_sums = (jnp.zeros((C, C), jnp.float32), jnp.zeros((C, C), jnp.float32))
        (real_sum, imag_sum), unused = lax.scan(add_slab, start_sums, jnp.arange(N_ROW, dtype=jnp.int32))
        weight = weight_table[chan_l[upper_id]][:, chan_l[lower_id]]
        upper_deg = (2 * jlevel[upper_id] + 1).astype(jnp.float32)
        lower_deg = (2 * jlevel[lower_id] + 1).astype(jnp.float32)
        factor = 2.0 * lower_deg / (upper_deg + lower_deg)
        results.append(factor * weight * real_sum)
        results.append(factor * weight * imag_sum)
    return jnp.stack(results)
```

```python
import functools

import jax
import jax.numpy as jnp
from jax import lax
from jax.experimental import pallas as pl
from jax.experimental.pallas import tpu as pltpu
from jax.sharding import PartitionSpec as P

MESH = pl.DeviceIdType.MESH
LANES = 128


def plan(rows, width):
    live = 14 * rows
    upper = 4 * rows
    main = live // LANES // 4 * LANES
    extra = live - 4 * main
    return live, upper, main, extra, main + extra


def kernel(
    rows, width, re_ref, im_ref, meta_ref, table_ref, out_ref,
    up, low, swapped, acc, other, ready, weight, zeros, meta,
    send_up, recv_up, send_low, recv_low, send_sum, recv_sum, send_out, recv_out, local_sem,
):
    live, upper, main, extra, lower = plan(rows, width)
    j, r = lax.axis_index("jpair"), lax.axis_index("row")
    pair, parity = j // 2, j % 2
    x, half, core = r // 4, (r // 2) % 2, r % 2
    y = 2 * half + parity
    is_upper, is_lower = parity == 0, parity == 1
    source = (re_ref, im_ref)

    def device(dx, dy, dcore=0):
        to_x, to_y = (x + dx) % 4, (y + dy) % 4
        return (2 * pair + to_y % 2, 4 * to_x + 2 * (to_y // 2) + (core + dcore) % 2)

    def remote(src, dst, send, recv, where):
        return pltpu.make_async_remote_copy(
            src_ref=src, dst_ref=dst, send_sem=send, recv_sem=recv, device_id=where, device_id_type=MESH
        )

    barrier = pltpu.get_barrier_semaphore()
    greeted = [(1, 0, 0), (3, 0, 0), (2, 0, 0), (0, 1, 0), (0, 3, 0), (0, 2, 0), (0, 0, 1)]
    for offset in greeted:
        pl.semaphore_signal(barrier, inc=1, device_id=device(*offset), device_id_type=MESH)
    pl.semaphore_wait(barrier, len(greeted))

    def slab_at(dx, dhalf):
        return 2 * ((x + dx) % 4) + (half + dhalf) % 2

    def piece(buffer, slab, part):
        return buffer.at[pl.ds(pl.multiple_of(slab * (2 * rows) + part * rows, rows), rows)]

    pending = []

    def send(when, copy):
        pl.when(when)(copy.start)
        pending.append((when, copy))

    def arrived(when, buffer, sems, slab, part):
        @pl.when(when)
        def _():
            here = piece(buffer, slab, part)
            remote(here, here, send_up.at[0], sems.at[slab, part], device(1, 0)).wait_recv()

    my_slab = slab_at(0, 0)
    have_rows = my_slab < 7
    up_from = is_upper & have_rows
    low_from = is_lower & have_rows

    partner = device(0, 1 - 2 * parity)
    meta_copy = remote(meta_ref, meta.at[pl.ds(0, 1)], local_sem.at[0], local_sem.at[1], partner)
    meta_copy.start()

    def up_columns(part, to_x):
        return source[part].at[0, :, pl.ds(pl.multiple_of(to_x * upper, LANES), upper)]

    def low_columns(part, to_y):
        return source[part].at[0, :, pl.ds(pl.multiple_of(to_y * main, LANES), lower)]

    for part in range(2):
        for n, dy in enumerate((1, 3)):
            send(up_from, remote(
                up_columns(part, x), piece(up, my_slab, part),
                send_up.at[6 + 2 * n + part], recv_up.at[my_slab, part], device(0, dy)))
    for n, dx in enumerate((1, 3, 2)):
        for part in range(2):
            send(up_from, remote(
                up_columns(part, (x + dx) % 4), piece(up, my_slab, part),
                send_up.at[2 * n + part], recv_up.at[my_slab, part], device(dx, 0)))
    for n, dy in enumerate((1, 3, 2)):
        for part in range(2):
            send(low_from, remote(
                low_columns(part, (y + dy) % 4), piece(low, my_slab, part),
                send_low.at[2 * n + part], recv_low.at[my_slab, part], device(0, dy)))
    for part in range(2):
        for n, dx in enumerate((1, 3)):
            send(low_from, remote(
                low_columns(part, y), piece(low, my_slab, part),
                send_low.at[6 + 2 * n + part], recv_low.at[my_slab, part], device(dx, 0)))

    own = []
    for part in range(2):
        own.append((up_from, pltpu.make_async_copy(
            up_columns(part, x), piece(up, my_slab, part), local_sem.at[2 + part])))
        own.append((low_from, pltpu.make_async_copy(
            low_columns(part, y), piece(low, my_slab, part), local_sem.at[2 + part])))
    for when, copy in own:
        pl.when(when)(copy.start)

    zeros[...] = jnp.zeros_like(zeros)
    fills = [(pl.program_id(0) == 0, width - 2 * rows)]
    fills += [(my_slab == 7, n * 2 * rows) for n in range(7)]
    blank = []
    for n, (when, start) in enumerate(fills):
        blank.append((when, pltpu.make_async_copy(
            zeros, out_ref.at[0, :, pl.ds(start, 2 * rows)], local_sem.at[4 + n])))
    for when, copy in blank:
        pl.when(when)(copy.start)
    acc[...] = jnp.zeros_like(acc)

    meta_copy.wait()
    mine, theirs = meta_ref[...], meta[0:1, :]
    first = jnp.where(is_upper, mine, theirs)
    second = jnp.where(is_upper, theirs, mine)
    upper_count, lower_count = first[:, width:width + 1], second[:, width:width + 1]
    upper_deg = (2 * first[:, width + LANES:width + LANES + 1] + 1).astype(jnp.float32)
    lower_deg = (2 * second[:, width + LANES:width + LANES + 1] + 1).astype(jnp.float32)
    factor = 2.0 * lower_deg / (upper_deg + lower_deg)
    meta[1:2, :] = first
    meta[2:3, :] = second
    levels = table_ref.shape[0]
    c_start = pl.multiple_of(x * upper, LANES)
    d_start = pl.multiple_of(y * main, LANES)
    c_labels = meta[1:2, pl.ds(c_start, upper)]
    d_labels = meta[2:3, pl.ds(d_start, lower)]
    c_open = c_start + lax.broadcasted_iota(jnp.int32, (1, upper), 1) < upper_count
    d_open = d_start + lax.broadcasted_iota(jnp.int32, (1, lower), 1) < lower_count
    c_labels = jnp.where(c_open, c_labels, -1)
    d_labels = jnp.where(d_open, d_labels, -1)
    c_hot = (lax.broadcasted_iota(jnp.int32, (levels, upper), 0) == c_labels).astype(jnp.float32)
    d_hot = (lax.broadcasted_iota(jnp.int32, (levels, lower), 0) == d_labels).astype(jnp.float32)
    picked = factor * jnp.dot(
        table_ref[...], d_hot, precision=lax.Precision.HIGHEST, preferred_element_type=jnp.float32)
    weight[...] = lax.dot_general(
        c_hot, picked, (((0,), (0,)), ((), ())),
        precision=lax.Precision.HIGHEST, preferred_element_type=jnp.float32)
    least = jnp.minimum(upper_count, lower_count)
    for when, copy in own:
        pl.when(when)(copy.wait)

    tile = min(256, upper)

    def accumulate(slab):
        @pl.when(slab < 7)
        def _():
            row = pl.multiple_of(slab * 2 * rows, rows)
            first_row = (slab // 2) * (4 * rows) + (slab % 2) * (2 * rows) + core * rows
            row_ids = first_row + lax.broadcasted_iota(jnp.int32, (rows, lower), 0)
            keep = (row_ids < least).astype(jnp.float32).astype(jnp.bfloat16)
            low_re = low[pl.ds(row, rows)] * keep
            low_im = low[pl.ds(pl.multiple_of(row + rows, rows), rows)] * keep
            swapped[0, :rows] = low_re
            swapped[0, rows:] = low_im
            swapped[1, :rows] = low_im
            swapped[1, rows:] = -low_re

            @pl.loop(0, upper // tile)
            def _(n):
                start = pl.multiple_of(n * tile, tile)
                left = up[pl.ds(row, 2 * rows), pl.ds(start, tile)]
                for part in range(2):
                    acc[part, pl.ds(start, tile)] += lax.dot_general(
                        left, swapped[part], (((0,), (0,)), ((), ())), preferred_element_type=jnp.float32)

    used = {"up": 10, "low": 10}

    def on_up(when, slab, part, dy):
        n = used["up"]
        used["up"] += 1
        here = piece(up, slab, part)
        send(when, remote(here, here, send_up.at[n], recv_up.at[slab, part], device(0, dy)))

    def on_low(when, slab, part, dx):
        n = used["low"]
        used["low"] += 1
        here = piece(low, slab, part)
        send(when, remote(here, here, send_low.at[n], recv_low.at[slab, part], device(dx, 0)))

    def own_low(dhalf):
        slab = slab_at(0, dhalf)
        when = (is_upper if dhalf == 0 else (slab >= 0)) & (slab < 7)
        for part in range(2):
            arrived(when, low, recv_low, slab, part)
            for dx in (1, 3):
                on_low(when, slab, part, dx)

    def next_low(dx, dhalf):
        slab = slab_at(dx, dhalf)
        when = slab < 7
        first_part = 0 if dx == 3 else 1
        for part in (first_part, 1 - first_part):
            arrived(when, low, recv_low, slab, part)
            if part == first_part:
                on_low(when, slab, part, 4 - dx)

    def far_low(dhalf):
        slab = slab_at(2, dhalf)
        for part in range(2):
            arrived(slab < 7, low, recv_low, slab, part)

    def even_up(dx):
        slab = slab_at(dx, 0)
        when = is_upper & (slab < 7)
        for part in range(2):
            arrived(when, up, recv_up, slab, part)
            for dy in (1, 3):
                on_up(when, slab, part, dy)

    def odd_up(dx):
        for dy, dhalf in ((3, 0), (1, 1)):
            slab = slab_at(dx, dhalf)
            when = is_lower & (slab < 7)
            first_part = 0 if dy == 3 else 1
            for part in (first_part, 1 - first_part):
                arrived(when, up, recv_up, slab, part)
                if part == first_part:
                    on_up(when, slab, part, 4 - dy)

    def far_up(dx):
        slab = slab_at(dx, 1)
        for part in range(2):
            arrived(is_upper & (slab < 7), up, recv_up, slab, part)

    odd_up(0)
    own_low(0)
    own_low(1)
    accumulate(slab_at(0, 0))
    even_up(1)
    even_up(3)
    next_low(1, 0)
    next_low(3, 0)
    next_low(1, 1)
    next_low(3, 1)
    odd_up(1)
    odd_up(3)
    even_up(2)
    far_up(0)
    accumulate(slab_at(0, 1))
    accumulate(slab_at(1, 0))
    accumulate(slab_at(3, 0))
    odd_up(2)
    far_up(1)
    accumulate(slab_at(1, 1))
    far_up(3)
    accumulate(slab_at(3, 1))
    far_low(0)
    accumulate(slab_at(2, 0))
    far_low(1)
    far_up(2)
    accumulate(slab_at(2, 1))

    order = (2, 1, 3, 0)

    def rows_of(to_y, of_core):
        return pl.ds(pl.multiple_of((to_y // 2) * (2 * rows) + of_core * rows, rows), rows)

    sums = []
    for n, dy in enumerate(order):
        to_y = (y + dy) % 4
        when = (x < 3) | (to_y < 2)
        copy = remote(
            acc.at[to_y % 2, rows_of(to_y, 1 - core)], other.at[n], send_sum.at[n], recv_sum.at[n], device(0, 0, 1))
        pl.when(when)(copy.start)
        sums.append((when, copy))

    def out_copy(n, dy, start, count, sems, last):
        dst = out_ref.at[0, :, pl.ds(start, count)]
        src = ready.at[n, :, pl.ds(last, count)]
        return src, dst

    finish = []
    for n, dy in enumerate(order):
        to_y = (y + dy) % 4
        when, copy = sums[n]
        main_src = ready.at[n, :, pl.ds(0, main)]
        main_dst = out_ref.at[0, :, pl.ds(d_start, main)]
        extra_src = ready.at[n, :, pl.ds(main, extra)]
        extra_dst = out_ref.at[0, :, pl.ds(4 * main, extra)]
        if dy == 0:
            copies = [
                (when, pltpu.make_async_copy(main_src, main_dst, local_sem.at[12])),
                (when & (y == 3), pltpu.make_async_copy(extra_src, extra_dst, local_sem.at[13])),
            ]
        else:
            copies = [
                (when, remote(main_src, main_dst, send_out.at[0, n], recv_out.at[0, y], device(0, dy))),
                (when & (y == 3), remote(extra_src, extra_dst, send_out.at[1, n], recv_out.at[1, y], device(0, dy))),
            ]

        @pl.when(when)
        def _(n=n, to_y=to_y, copy=copy):
            copy.wait_recv()
            keep = rows_of(to_y, core)
            ready[n] = weight[keep] * (acc[to_y % 2, keep] + other[n])

        for start_when, out in copies:
            pl.when(start_when)(out.start)
        finish.append((dy, copies))

    for when, copy in pending:
        pl.when(when)(copy.wait_send)
    for when, copy in sums:
        pl.when(when)(copy.wait_send)
    for when, copy in blank:
        pl.when(when)(copy.wait)
    get = (x < 3) | (half == 0)
    for dy, copies in finish:
        for when, copy in copies:
            pl.when(when)(copy.wait if dy == 0 else copy.wait_send)
    for dy in (1, 3, 2):
        from_y = (y + dy) % 4

        @pl.when(get)
        def _(from_y=from_y):
            here = out_ref.at[0, :, pl.ds(pl.multiple_of(from_y * main, LANES), main)]
            remote(here, here, send_out.at[0, 0], recv_out.at[0, from_y], device(1, 0)).wait_recv()

        @pl.when(get & (from_y == 3))
        def _(from_y=from_y):
            here = out_ref.at[0, :, pl.ds(4 * main, extra)]
            remote(here, here, send_out.at[1, 0], recv_out.at[1, from_y], device(1, 0)).wait_recv()


def per_device(s_real, s_imag, chan_l, counts, jlevel, allowed, recoup):
    rows, width = s_real.shape[1:]
    live, upper, main, extra, lower = plan(rows, width)
    table = recoup * allowed.astype(jnp.float32)
    meta = jnp.concatenate([
        chan_l, jnp.broadcast_to(counts[:, None], (1, LANES)), jnp.broadcast_to(jlevel[:, None], (1, LANES))], 1)
    vmem = pl.BlockSpec(memory_space=pltpu.VMEM)
    dma = pltpu.SemaphoreType.DMA
    return pl.pallas_call(
        functools.partial(kernel, rows, width),
        grid=(1,),
        out_shape=jax.ShapeDtypeStruct((1, rows, width), jnp.float32),
        in_specs=[vmem] * 4,
        out_specs=pl.BlockSpec(memory_space=pl.ANY),
        scratch_shapes=[
            pltpu.VMEM((14 * rows, upper), jnp.bfloat16),
            pltpu.VMEM((14 * rows, lower), jnp.bfloat16),
            pltpu.VMEM((2, 2 * rows, lower), jnp.bfloat16),
            pltpu.VMEM((2, upper, lower), jnp.float32),
            pltpu.VMEM((4, rows, lower), jnp.float32),
            pltpu.VMEM((4, rows, lower), jnp.float32),
            pltpu.VMEM((upper, lower), jnp.float32),
            pltpu.VMEM((rows, 2 * rows), jnp.float32),
            pltpu.VMEM((8, width + 2 * LANES), jnp.int32),
            dma((64,)), dma((7, 2)), dma((64,)), dma((7, 2)),
            dma((4,)), dma((4,)), dma((2, 4)), dma((2, 4)), dma((16,)),
        ],
        compiler_params=pltpu.CompilerParams(
            collective_id=0, has_side_effects=True, vmem_limit_bytes=48 << 20),
        cost_estimate=pl.CostEstimate(
            flops=16 * 7 * rows * upper * lower, bytes_accessed=8 * rows * width, transcendentals=0),
    )(s_real, s_imag, meta, table)


def solution(mesh):
    placed = (
        P("jpair", "row", None),
        P("jpair", "row", None),
        P("jpair", None),
        P("jpair"),
        P("jpair"),
        P(),
        P(),
    )
    return jax.shard_map(
        per_device, mesh=mesh, in_specs=placed, out_specs=P("jpair", "row", None), check_vma=False
    )
```

```python
import functools

import jax
import jax.numpy as jnp
from jax import lax
from jax.experimental import pallas as pl
from jax.experimental.pallas import tpu as pltpu
from jax.sharding import PartitionSpec as P

MESH = pl.DeviceIdType.MESH
LANES = 128


def plan(rows, width):
    live = 14 * rows
    upper = 4 * rows
    main = live // LANES // 4 * LANES
    extra = live - 4 * main
    return live, upper, main, extra, main + extra


def kernel(
    rows, width, re_ref, im_ref, chan_ref, count_ref, level_ref, allowed_ref, recoup_ref, out_ref,
    up, low, swapped, acc, other, ready, weight, zeros, mine, theirs, labels,
    send_up, recv_up, send_low, recv_low, send_sum, recv_sum, send_out, recv_out, local_sem,
):
    live, upper, main, extra, lower = plan(rows, width)
    j, r = lax.axis_index("jpair"), lax.axis_index("row")
    pair, parity = j // 2, j % 2
    x, half, core = r // 4, (r // 2) % 2, r % 2
    y = 2 * half + parity
    is_upper, is_lower = parity == 0, parity == 1
    source = (re_ref, im_ref)

    def device(dx, dy, dcore=0):
        to_x, to_y = (x + dx) % 4, (y + dy) % 4
        return (2 * pair + to_y % 2, 4 * to_x + 2 * (to_y // 2) + (core + dcore) % 2)

    def remote(src, dst, send, recv, where):
        return pltpu.make_async_remote_copy(
            src_ref=src, dst_ref=dst, send_sem=send, recv_sem=recv, device_id=where, device_id_type=MESH
        )

    barrier = pltpu.get_barrier_semaphore()
    greeted = [(1, 0, 0), (3, 0, 0), (2, 0, 0), (0, 1, 0), (0, 3, 0), (0, 2, 0), (0, 0, 1)]
    for offset in greeted:
        pl.semaphore_signal(barrier, inc=1, device_id=device(*offset), device_id_type=MESH)
    pl.semaphore_wait(barrier, len(greeted))

    def slab_at(dx, dhalf):
        return 2 * ((x + dx) % 4) + (half + dhalf) % 2

    def piece(buffer, slab, part, count):
        return buffer.at[pl.ds(pl.multiple_of(slab * (2 * rows) + part * rows, rows), rows), pl.ds(0, count)]

    pending = []

    def send(when, copy):
        pl.when(when)(copy.start)
        pending.append((when, copy))

    def arrived(when, buffer, slab, part):
        here_up = buffer is up
        sems = recv_up if here_up else recv_low
        sizes = ((x < 3, upper), (x == 3, 2 * rows)) if here_up else ((y < 3, main), (y == 3, lower))
        for size_when, count in sizes:
            @pl.when(when & size_when)
            def _(count=count):
                here = piece(buffer, slab, part, count)
                remote(here, here, send_up.at[0], sems.at[slab, part], device(1, 0)).wait_recv()

    my_slab = slab_at(0, 0)
    have_rows = my_slab < 7
    up_from = is_upper & have_rows
    low_from = is_lower & have_rows

    mine[:, :width] = chan_ref[...]
    mine[:, width:width + LANES] = jnp.broadcast_to(count_ref[...], (1, LANES))
    mine[:, width + LANES:] = jnp.broadcast_to(level_ref[...], (1, LANES))
    meta_copy = remote(mine, theirs, local_sem.at[0], local_sem.at[1], device(0, 1 - 2 * parity))
    meta_copy.start()

    def send_up_piece(when, to_x, src, part, n, slab, where):
        for narrow, count in ((False, upper), (True, 2 * rows)):
            send(when & ((to_x == 3) if narrow else (to_x < 3)), remote(
                src(count), piece(up, slab, part, count), send_up.at[n], recv_up.at[slab, part], where))

    def send_low_piece(when, to_y, src, part, n, slab, where):
        for wide, count in ((False, main), (True, lower)):
            send(when & ((to_y == 3) if wide else (to_y < 3)), remote(
                src(count), piece(low, slab, part, count), send_low.at[n], recv_low.at[slab, part], where))

    def up_columns(part, to_x):
        return lambda count: source[part].at[0, :, pl.ds(pl.multiple_of(to_x * upper, LANES), count)]

    def low_columns(part, to_y):
        return lambda count: source[part].at[0, :, pl.ds(pl.multiple_of(to_y * main, LANES), count)]

    for part in range(2):
        for n, dy in enumerate((1, 3)):
            send_up_piece(up_from, x, up_columns(part, x), part, 6 + 2 * n + part, my_slab, device(0, dy))
    for n, dx in enumerate((1, 3, 2)):
        for part in range(2):
            to_x = (x + dx) % 4
            send_up_piece(up_from, to_x, up_columns(part, to_x), part, 2 * n + part, my_slab, device(dx, 0))
    for n, dy in enumerate((1, 3, 2)):
        for part in range(2):
            to_y = (y + dy) % 4
            send_low_piece(low_from, to_y, low_columns(part, to_y), part, 2 * n + part, my_slab, device(0, dy))
    for part in range(2):
        for n, dx in enumerate((1, 3)):
            send_low_piece(low_from, y, low_columns(part, y), part, 6 + 2 * n + part, my_slab, device(dx, 0))

    own = []
    for part in range(2):
        own.append((up_from, pltpu.make_async_copy(
            up_columns(part, x)(upper), piece(up, my_slab, part, upper), local_sem.at[2 + part])))
        own.append((low_from, pltpu.make_async_copy(
            low_columns(part, y)(lower), piece(low, my_slab, part, lower), local_sem.at[2 + part])))
    for when, copy in own:
        pl.when(when)(copy.start)

    zeros[...] = jnp.zeros_like(zeros)
    fills = [(pl.program_id(0) == 0, width - 2 * rows)]
    fills += [(my_slab == 7, n * 2 * rows) for n in range(7)]
    blank = []
    for n, (when, start) in enumerate(fills):
        blank.append((when, pltpu.make_async_copy(
            zeros, out_ref.at[0, :, pl.ds(start, 2 * rows)], local_sem.at[4 + n])))
    for when, copy in blank:
        pl.when(when)(copy.start)
    acc[...] = jnp.zeros_like(acc)

    meta_copy.wait()
    first = jnp.where(is_upper, mine[...], theirs[...])
    second = jnp.where(is_upper, theirs[...], mine[...])
    upper_count, lower_count = first[:, width:width + 1], second[:, width:width + 1]
    upper_deg = (2 * first[:, width + LANES:width + LANES + 1] + 1).astype(jnp.float32)
    lower_deg = (2 * second[:, width + LANES:width + LANES + 1] + 1).astype(jnp.float32)
    factor = 2.0 * lower_deg / (upper_deg + lower_deg)
    labels[0:1, :] = first
    labels[1:2, :] = second
    table = recoup_ref[...] * allowed_ref[...].astype(jnp.float32)
    levels = table.shape[0]
    c_start = pl.multiple_of(x * upper, LANES)
    d_start = pl.multiple_of(y * main, LANES)
    c_labels = labels[0:1, pl.ds(c_start, upper)]
    d_labels = labels[1:2, pl.ds(d_start, lower)]
    c_open = c_start + lax.broadcasted_iota(jnp.int32, (1, upper), 1) < upper_count
    d_open = d_start + lax.broadcasted_iota(jnp.int32, (1, lower), 1) < lower_count
    c_labels = jnp.where(c_open, c_labels, -1)
    d_labels = jnp.where(d_open, d_labels, -1)
    c_hot = (lax.broadcasted_iota(jnp.int32, (levels, upper), 0) == c_labels).astype(jnp.float32)
    d_hot = (lax.broadcasted_iota(jnp.int32, (levels, lower), 0) == d_labels).astype(jnp.float32)
    picked = factor * jnp.dot(
        table, d_hot, precision=lax.Precision.HIGHEST, preferred_element_type=jnp.float32)
    weight[...] = lax.dot_general(
        c_hot, picked, (((0,), (0,)), ((), ())),
        precision=lax.Precision.HIGHEST, preferred_element_type=jnp.float32)
    least = jnp.minimum(upper_count, lower_count)
    for when, copy in own:
        pl.when(when)(copy.wait)

    tile = min(256, upper)

    def accumulate(slab):
        @pl.when(slab < 7)
        def _():
            row = pl.multiple_of(slab * 2 * rows, rows)
            first_row = (slab // 2) * (4 * rows) + (slab % 2) * (2 * rows) + core * rows
            row_ids = first_row + lax.broadcasted_iota(jnp.int32, (rows, lower), 0)
            keep = (row_ids < least).astype(jnp.float32).astype(jnp.bfloat16)
            low_re = low[pl.ds(row, rows)] * keep
            low_im = low[pl.ds(pl.multiple_of(row + rows, rows), rows)] * keep
            swapped[0, :rows] = low_re
            swapped[0, rows:] = low_im
            swapped[1, :rows] = low_im
            swapped[1, rows:] = -low_re

            @pl.loop(0, upper // tile)
            def _(n):
                start = pl.multiple_of(n * tile, tile)
                left = up[pl.ds(row, 2 * rows), pl.ds(start, tile)]
                for part in range(2):
                    acc[part, pl.ds(start, tile)] += lax.dot_general(
                        left, swapped[part], (((0,), (0,)), ((), ())), preferred_element_type=jnp.float32)

    used = {"up": 10, "low": 10}

    def on_up(when, slab, part, dy):
        send_up_piece(when, x, lambda count: piece(up, slab, part, count), part, used["up"], slab, device(0, dy))
        used["up"] += 1

    def on_low(when, slab, part, dx):
        send_low_piece(when, y, lambda count: piece(low, slab, part, count), part, used["low"], slab, device(dx, 0))
        used["low"] += 1

    def own_low(dhalf):
        slab = slab_at(0, dhalf)
        when = (is_upper if dhalf == 0 else (slab >= 0)) & (slab < 7)
        for part in range(2):
            arrived(when, low, slab, part)
            for dx in (1, 3):
                on_low(when, slab, part, dx)

    def next_low(side, dx, dhalf):
        slab = slab_at(dx, dhalf)
        when = side & (slab < 7)
        first_part = 0 if dx == 3 else 1
        for part in (first_part, 1 - first_part):
            arrived(when, low, slab, part)
            if part == first_part:
                on_low(when, slab, part, 4 - dx)

    def far_low(dhalf):
        slab = slab_at(2, dhalf)
        for part in range(2):
            arrived(slab < 7, low, slab, part)

    def even_up(dx):
        slab = slab_at(dx, 0)
        when = is_upper & (slab < 7)
        for part in range(2):
            arrived(when, up, slab, part)
            for dy in (1, 3):
                on_up(when if dy == 1 + 2 * part else when & (slab < 6), slab, part, dy)

    def odd_up(dx):
        for dy, dhalf, part in ((3, 0, 0), (1, 1, 1)):
            slab = slab_at(dx, dhalf)
            when = is_lower & (slab < 7)
            arrived(when, up, slab, part)
            on_up(when, slab, part, 4 - dy)

    def odd_rest(dx, dhalf):
        slab = slab_at(dx, dhalf)
        arrived(is_lower & (slab < 7), up, slab, 1 - dhalf)

    def far_up(dx):
        slab = slab_at(dx, 1)
        for part in range(2):
            arrived(is_upper & (slab < 7), up, slab, part)
            if dx != 0:
                on_up(is_upper & (slab == 6), slab, part, 1 + 2 * part)

    odd_up(0)
    own_low(0)
    own_low(1)
    next_low(is_lower, 1, 0)
    next_low(is_lower, 3, 0)
    even_up(1)
    even_up(3)
    odd_rest(0, 0)
    accumulate(slab_at(0, 0))
    odd_up(1)
    odd_up(3)
    even_up(2)
    far_up(0)
    next_low(is_upper, 1, 0)
    next_low(is_upper, 3, 0)
    next_low(is_lower, 1, 1)
    next_low(is_lower, 3, 1)
    odd_rest(0, 1)
    accumulate(slab_at(0, 1))
    odd_rest(1, 0)
    accumulate(slab_at(1, 0))
    odd_rest(3, 0)
    accumulate(slab_at(3, 0))
    next_low(is_upper, 1, 1)
    next_low(is_upper, 3, 1)
    odd_up(2)
    far_up(1)
    odd_rest(1, 1)
    accumulate(slab_at(1, 1))
    far_up(3)
    odd_rest(3, 1)
    accumulate(slab_at(3, 1))
    far_low(0)
    odd_rest(2, 0)
    accumulate(slab_at(2, 0))
    far_low(1)
    far_up(2)
    odd_rest(2, 1)
    accumulate(slab_at(2, 1))

    order = (2, 1, 3, 0)

    def rows_of(to_y, of_core):
        return pl.ds(pl.multiple_of((to_y // 2) * (2 * rows) + of_core * rows, rows), rows)

    sums = []
    for n, dy in enumerate(order):
        to_y = (y + dy) % 4
        when = (x < 3) | (to_y < 2)
        copy = remote(
            acc.at[to_y % 2, rows_of(to_y, 1 - core)], other.at[n], send_sum.at[n], recv_sum.at[n], device(0, 0, 1))
        pl.when(when)(copy.start)
        sums.append((when, copy))

    finish = []
    for n, dy in enumerate(order):
        to_y = (y + dy) % 4
        when, copy = sums[n]
        main_src = ready.at[n, :, pl.ds(0, main)]
        main_dst = out_ref.at[0, :, pl.ds(d_start, main)]
        extra_src = ready.at[n, :, pl.ds(main, extra)]
        extra_dst = out_ref.at[0, :, pl.ds(4 * main, extra)]
        if dy == 0:
            copies = [
                (when, pltpu.make_async_copy(main_src, main_dst, local_sem.at[12])),
                (when & (y == 3), pltpu.make_async_copy(extra_src, extra_dst, local_sem.at[13])),
            ]
        else:
            copies = [
                (when, remote(main_src, main_dst, send_out.at[0, n], recv_out.at[0, y], device(0, dy))),
                (when & (y == 3), remote(extra_src, extra_dst, send_out.at[1, n], recv_out.at[1, y], device(0, dy))),
            ]

        @pl.when(when)
        def _(n=n, to_y=to_y, copy=copy):
            copy.wait_recv()
            keep = rows_of(to_y, core)
            ready[n] = weight[keep] * (acc[to_y % 2, keep] + other[n])

        for start_when, out in copies:
            pl.when(start_when)(out.start)
        finish.append((dy, copies))

    for when, copy in pending:
        pl.when(when)(copy.wait_send)
    for when, copy in sums:
        pl.when(when)(copy.wait_send)
    for when, copy in blank:
        pl.when(when)(copy.wait)
    get = (x < 3) | (half == 0)
    for dy, copies in finish:
        for when, copy in copies:
            pl.when(when)(copy.wait if dy == 0 else copy.wait_send)
    for dy in (1, 3, 2):
        from_y = (y + dy) % 4

        @pl.when(get)
        def _(from_y=from_y):
            here = out_ref.at[0, :, pl.ds(pl.multiple_of(from_y * main, LANES), main)]
            remote(here, here, send_out.at[0, 0], recv_out.at[0, from_y], device(1, 0)).wait_recv()

        @pl.when(get & (from_y == 3))
        def _(from_y=from_y):
            here = out_ref.at[0, :, pl.ds(4 * main, extra)]
            remote(here, here, send_out.at[1, 0], recv_out.at[1, from_y], device(1, 0)).wait_recv()


def per_device(s_real, s_imag, chan_l, counts, jlevel, allowed, recoup):
    rows, width = s_real.shape[1:]
    live, upper, main, extra, lower = plan(rows, width)
    vmem = pl.BlockSpec(memory_space=pltpu.VMEM)
    dma = pltpu.SemaphoreType.DMA
    return pl.pallas_call(
        functools.partial(kernel, rows, width),
        grid=(1,),
        out_shape=jax.ShapeDtypeStruct((1, rows, width), jnp.float32),
        in_specs=[pl.BlockSpec(memory_space=pl.ANY)] * 2 + [vmem] * 5,
        out_specs=pl.BlockSpec(memory_space=pl.ANY),
        scratch_shapes=[
            pltpu.VMEM((14 * rows, upper), jnp.bfloat16),
            pltpu.VMEM((14 * rows, lower), jnp.bfloat16),
            pltpu.VMEM((2, 2 * rows, lower), jnp.bfloat16),
            pltpu.VMEM((2, upper, lower), jnp.float32),
            pltpu.VMEM((4, rows, lower), jnp.float32),
            pltpu.VMEM((4, rows, lower), jnp.float32),
            pltpu.VMEM((upper, lower), jnp.float32),
            pltpu.VMEM((rows, 2 * rows), jnp.float32),
            pltpu.VMEM((1, width + 2 * LANES), jnp.int32),
            pltpu.VMEM((1, width + 2 * LANES), jnp.int32),
            pltpu.VMEM((8, width + 2 * LANES), jnp.int32),
            dma((64,)), dma((7, 2)), dma((64,)), dma((7, 2)),
            dma((4,)), dma((4,)), dma((2, 4)), dma((2, 4)), dma((16,)),
        ],
        compiler_params=pltpu.CompilerParams(
            collective_id=0, has_side_effects=True, vmem_limit_bytes=60 << 20),
        cost_estimate=pl.CostEstimate(
            flops=16 * 7 * rows * upper * lower, bytes_accessed=8 * rows * width, transcendentals=0),
    )(s_real, s_imag, chan_l, counts[:, None], jlevel[:, None], allowed, recoup)


def solution(mesh):
    placed = (
        P("jpair", "row", None),
        P("jpair", "row", None),
        P("jpair", None),
        P("jpair"),
        P("jpair"),
        P(),
        P(),
    )
    return jax.shard_map(
        per_device, mesh=mesh, in_specs=placed, out_specs=P("jpair", "row", None), check_vma=False
    )
```

```python
import functools

import jax
import jax.numpy as jnp
from jax import lax
from jax.experimental import pallas as pl
from jax.experimental.pallas import tpu as pltpu
from jax.sharding import PartitionSpec as P

MESH = pl.DeviceIdType.MESH
LANES = 128
RELAY, UPPER, LOWER, SUM = range(4)
ORDER = (
    (
        (RELAY, 0), (RELAY, 1), (UPPER, 1, 0, 0), (UPPER, 3, 0, 0), (LOWER, 0, 1, 0), (LOWER, 0, 0, 0),
        (UPPER, 1, 0, 1), (LOWER, 0, 1, 1), (LOWER, 0, 0, 1), (SUM, 0, 0), (UPPER, 3, 0, 1), (SUM, 0, 1),
        (UPPER, 2, 0, 0), (LOWER, 3, 1, 0), (LOWER, 3, 0, 0), (UPPER, 2, 0, 1), (LOWER, 1, 1, 1), (SUM, 3, 1),
        (LOWER, 1, 0, 1), (SUM, 1, 0), (SUM, 3, 0), (SUM, 1, 1), (SUM, 2, 1), (SUM, 2, 0),
    ),
    (
        (LOWER, 3, 0, 0), (UPPER, 0, 0, 0), (UPPER, 0, 1, 1), (LOWER, 1, 0, 1), (LOWER, 0, 1, 0), (LOWER, 0, 1, 1),
        (SUM, 0, 1), (UPPER, 1, 0, 0), (LOWER, 3, 1, 0), (UPPER, 1, 1, 1), (UPPER, 3, 0, 0), (LOWER, 1, 1, 1),
        (SUM, 1, 1), (SUM, 1, 0), (UPPER, 3, 1, 1), (SUM, 3, 0), (SUM, 3, 1), (UPPER, 2, 0, 0), (UPPER, 2, 1, 1),
        (SUM, 0, 0), (SUM, 2, 0), (SUM, 2, 1),
    ),
    (
        (RELAY, 1), (RELAY, 0), (UPPER, 1, 0, 0), (UPPER, 3, 0, 0), (LOWER, 0, 0, 0), (LOWER, 0, 1, 0),
        (UPPER, 1, 0, 1), (UPPER, 3, 0, 1), (LOWER, 0, 0, 1), (SUM, 0, 0), (LOWER, 0, 1, 1), (UPPER, 0, 1, 1),
        (UPPER, 0, 1, 0), (SUM, 0, 1), (UPPER, 2, 0, 0), (LOWER, 3, 0, 0), (LOWER, 1, 0, 1), (SUM, 1, 0),
        (LOWER, 3, 1, 0), (UPPER, 2, 0, 1), (LOWER, 1, 1, 1), (SUM, 3, 0), (SUM, 1, 1), (SUM, 3, 1), (SUM, 2, 0),
        (SUM, 2, 1),
    ),
    (
        (UPPER, 0, 0, 0), (UPPER, 0, 1, 1), (LOWER, 3, 0, 0), (SUM, 0, 0), (LOWER, 1, 0, 1), (LOWER, 0, 1, 1),
        (LOWER, 0, 1, 0), (UPPER, 1, 1, 1), (UPPER, 1, 0, 0), (UPPER, 3, 0, 0), (UPPER, 3, 1, 1), (SUM, 1, 0),
        (LOWER, 3, 1, 0), (SUM, 3, 0), (UPPER, 2, 0, 0), (LOWER, 1, 1, 1), (SUM, 1, 1), (SUM, 3, 1),
        (UPPER, 2, 1, 1), (SUM, 0, 1), (SUM, 2, 0), (SUM, 2, 1),
    ),
)


def plan(rows, width):
    live = 14 * rows
    upper = 4 * rows
    main = live // LANES // 4 * LANES
    extra = live - 4 * main
    return live, upper, main, extra, main + extra


def kernel(
    rows, width, re_ref, im_ref, chan_ref, count_ref, level_ref, allowed_ref, recoup_ref, out_ref,
    up, low, transit, swapped, acc, other, coded, got, gain, got_gain, weight, mine, theirs, labels,
    send_up, recv_up, send_low, recv_low, recv_transit, send_sum, recv_sum, send_out, recv_out, local_sem,
):
    live, upper, main, extra, lower = plan(rows, width)
    j, r = lax.axis_index("jpair"), lax.axis_index("row")
    pair, parity = j // 2, j % 2
    x, half, core = r // 4, (r // 2) % 2, r % 2
    y = 2 * half + parity
    is_upper, is_lower = parity == 0, parity == 1
    source = (re_ref, im_ref)

    def device(dx, dy, dcore=0):
        to_x, to_y = (x + dx) % 4, (y + dy) % 4
        return (2 * pair + to_y % 2, 4 * to_x + 2 * (to_y // 2) + (core + dcore) % 2)

    def remote(src, dst, send, recv, where):
        return pltpu.make_async_remote_copy(
            src_ref=src, dst_ref=dst, send_sem=send, recv_sem=recv, device_id=where, device_id_type=MESH
        )

    barrier = pltpu.get_barrier_semaphore()
    greeted = [(1, 0, 0), (3, 0, 0), (2, 0, 0), (0, 1, 0), (0, 3, 0), (0, 2, 0), (0, 0, 1)]
    for offset in greeted:
        pl.semaphore_signal(barrier, inc=1, device_id=device(*offset), device_id_type=MESH)
    pl.semaphore_wait(barrier, len(greeted))

    def slab_at(dx, dhalf):
        return 2 * ((x + dx) % 4) + (half + dhalf) % 2

    def piece(buffer, slab, part, count):
        return buffer.at[pl.ds(pl.multiple_of(slab * (2 * rows) + part * rows, rows), rows), pl.ds(0, count)]

    my_slab = slab_at(0, 0)
    have_rows = my_slab < 7
    up_from, low_from = is_upper & have_rows, is_lower & have_rows

    mine[:, :width] = chan_ref[...]
    mine[:, width:width + LANES] = jnp.broadcast_to(count_ref[...], (1, LANES))
    mine[:, width + LANES:] = jnp.broadcast_to(level_ref[...], (1, LANES))
    meta_copy = remote(mine, theirs, local_sem.at[0], local_sem.at[1], device(0, 1 - 2 * parity))
    meta_copy.start()

    def low_count(to_y):
        return lower if to_y % 4 == 3 else main

    def up_columns(part, to_x):
        return lambda count: source[part].at[0, :, pl.ds(pl.multiple_of(to_x * upper, LANES), count)]

    def low_columns(part, to_y, count):
        return source[part].at[0, :, pl.ds(pl.multiple_of(to_y * main, LANES), count)]

    pending = [[] for _ in range(4)]
    used = {"up": 0, "low": 0}

    def send(at_y, make):
        for when, copy in make():
            pl.when(when)(copy.start)
        pending[at_y].append(make)

    def send_up_piece(at_y, when, src, part, dx, dhalf, to):
        n = used["up"]
        used["up"] += 1

        def make():
            slab = slab_at(dx, dhalf)
            ok = (slab < 7) if when is None else (slab < 7) & when()
            to_x = (x + to[0]) % 4
            return [
                (ok & size_when, remote(
                    src(slab, count), piece(up, slab, part, count), send_up.at[n], recv_up.at[slab, part], device(*to)))
                for size_when, count in ((to_x < 3, upper), (to_x == 3, 2 * rows))]

        send(at_y, make)

    def send_low_piece(at_y, src, part, dx, dhalf, to, count, passing=False):
        n = used["low"]
        used["low"] += 1

        def make():
            slab = slab_at(dx, dhalf)
            if passing:
                dst, recv = transit.at[pl.ds(part * rows, rows), pl.ds(0, count)], recv_transit.at[part]
            else:
                dst, recv = piece(low, slab, part, count), recv_low.at[slab, part]
            return [(slab < 7, remote(src(slab), dst, send_low.at[n], recv, device(*to)))]

        send(at_y, make)

    def begin(at_y):
        used["up"] = used["low"] = 0
        if at_y % 2 == 0:
            for part, dy in ((0, 1), (1, 3), (0, 3), (1, 1)):
                when = (lambda: x == 3) if at_y == 0 and dy != 1 + 2 * part else None
                send_up_piece(at_y, when, lambda slab, count, part=part: up_columns(part, x)(count), part, 0, 0, (0, dy))
            for dx in (1, 3, 2):
                for part in range(2):
                    send_up_piece(
                        at_y, None, lambda slab, count, part=part, dx=dx: up_columns(part, (x + dx) % 4)(count),
                        part, 0, 0, (dx, 0))
        else:
            to = [(0, part, 1 + 2 * part, at_y + 2) for part in range(2)]
            to += [(0, part, dy, at_y + dy) for part in range(2) for dy in (1, 3)]
            to += [(dx, part, 0, at_y) for part in range(2) for dx in (1, 3)]
            for n, (dx, part, dy, to_y) in enumerate(to):
                count = low_count(to_y)
                send_low_piece(
                    at_y, lambda slab, part=part, to_y=to_y, count=count: low_columns(part, to_y % 4, count),
                    part, 0, 0, (dx, dy), count, passing=n < 2)
        marks.append(dict(used))

    marks = []
    for at_y in range(4):
        pl.when(y == at_y)(functools.partial(begin, at_y))

    own = []
    for part in range(2):
        own.append((up_from, pltpu.make_async_copy(
            up_columns(part, x)(upper), piece(up, my_slab, part, upper), local_sem.at[2 + part])))
        own.append((low_from, pltpu.make_async_copy(
            low_columns(part, y, lower), piece(low, my_slab, part, lower), local_sem.at[2 + part])))
    for when, copy in own:
        pl.when(when)(copy.start)

    out_ref[0, :, live:] = jnp.zeros((rows, width - live), jnp.float32)

    @pl.when(my_slab == 7)
    def _():
        out_ref[0, :, :live] = jnp.zeros((rows, live), jnp.float32)

    acc[...] = jnp.zeros_like(acc)

    meta_copy.wait()
    first = jnp.where(is_upper, mine[...], theirs[...])
    second = jnp.where(is_upper, theirs[...], mine[...])
    upper_count, lower_count = first[:, width:width + 1], second[:, width:width + 1]
    upper_deg = (2 * first[:, width + LANES:width + LANES + 1] + 1).astype(jnp.float32)
    lower_deg = (2 * second[:, width + LANES:width + LANES + 1] + 1).astype(jnp.float32)
    factor = 2.0 * lower_deg / (upper_deg + lower_deg)
    labels[0:1, :] = first
    labels[1:2, :] = second
    table = recoup_ref[...] * allowed_ref[...].astype(jnp.float32)
    levels = table.shape[0]
    c_start = pl.multiple_of(x * upper, LANES)
    d_start = pl.multiple_of(y * main, LANES)
    c_labels = labels[0:1, pl.ds(c_start, upper)]
    d_labels = labels[1:2, pl.ds(d_start, lower)]
    c_open = c_start + lax.broadcasted_iota(jnp.int32, (1, upper), 1) < upper_count
    d_open = d_start + lax.broadcasted_iota(jnp.int32, (1, lower), 1) < lower_count
    c_labels = jnp.where(c_open, c_labels, -1)
    d_labels = jnp.where(d_open, d_labels, -1)
    c_hot = (lax.broadcasted_iota(jnp.int32, (levels, upper), 0) == c_labels).astype(jnp.float32)
    d_hot = (lax.broadcasted_iota(jnp.int32, (levels, lower), 0) == d_labels).astype(jnp.float32)
    picked = factor * jnp.dot(
        table, d_hot, precision=lax.Precision.HIGHEST, preferred_element_type=jnp.float32)
    weight[...] = lax.dot_general(
        c_hot, picked, (((0,), (0,)), ((), ())),
        precision=lax.Precision.HIGHEST, preferred_element_type=jnp.float32)
    least = jnp.minimum(upper_count, lower_count)
    for when, copy in own:
        pl.when(when)(copy.wait)

    tile = min(256, upper)

    def accumulate(slab):
        @pl.when(slab < 7)
        def _():
            row = pl.multiple_of(slab * 2 * rows, rows)
            first_row = (slab // 2) * (4 * rows) + (slab % 2) * (2 * rows) + core * rows
            row_ids = first_row + lax.broadcasted_iota(jnp.int32, (rows, lower), 0)
            keep = (row_ids < least).astype(jnp.float32).astype(jnp.bfloat16)
            low_re = low[pl.ds(row, rows)] * keep
            low_im = low[pl.ds(pl.multiple_of(row + rows, rows), rows)] * keep
            swapped[0, :rows] = low_re
            swapped[0, rows:] = low_im
            swapped[1, :rows] = low_im
            swapped[1, rows:] = -low_re

            @pl.loop(0, upper // tile)
            def _(n):
                start = pl.multiple_of(n * tile, tile)
                left = up[pl.ds(row, 2 * rows), pl.ds(start, tile)]
                for part in range(2):
                    acc[part, pl.ds(start, tile)] += lax.dot_general(
                        left, swapped[part], (((0,), (0,)), ((), ())), preferred_element_type=jnp.float32)

    def wait_piece(at_y, kind, slab, part):
        if kind == UPPER:
            for size_when, count in ((x < 3, upper), (x == 3, 2 * rows)):
                here = piece(up, slab, part, count)
                pl.when((slab < 7) & size_when)(
                    remote(here, here, send_up.at[0], recv_up.at[slab, part], device(1, 0)).wait_recv)
        else:
            here = piece(low, slab, part, low_count(at_y))
            pl.when(slab < 7)(remote(here, here, send_low.at[0], recv_low.at[slab, part], device(1, 0)).wait_recv)

    def go_on(at_y, kind, dx, dhalf, part):
        if kind == LOWER:
            count = low_count(at_y)
            for to_dx in ((1, 3) if dx == 0 else (4 - dx,)):
                send_low_piece(
                    at_y, lambda slab: piece(low, slab, part, count), part, dx, dhalf, (to_dx, 0), count)
            return
        when = None
        if at_y % 2 == 1:
            hops = [(part, 1 + 2 * part)]
        elif dhalf == 1:
            hops = [(part, 1 + 2 * part)]
            when = lambda: x < 3
        elif part == 0:
            hops = [(0, 1)]
        else:
            hops = [(1, 3), (0, 3), (1, 1)]
        for of_part, dy in hops:
            send_up_piece(
                at_y, when, lambda slab, count, of_part=of_part: piece(up, slab, of_part, count),
                of_part, dx, dhalf, (0, dy))

    def relay(at_y, part):
        dy = 1 + 2 * part
        count = low_count(at_y + dy)
        here = transit.at[pl.ds(part * rows, rows), pl.ds(0, count)]
        pl.when(slab_at(0, 1 - part) < 7)(
            remote(here, here, send_low.at[0], recv_transit.at[part], device(1, 0)).wait_recv)
        send_low_piece(at_y, lambda slab: here, part, 0, 1 - part, (0, dy), count)

    def steps(at_y):
        cut = [[]]
        for event in ORDER[at_y]:
            cut[-1].append(event)
            if event[0] == SUM:
                cut.append([])
        return cut

    waited = [{(UPPER if at_y % 2 == 0 else LOWER, 0, 0, part) for part in range(2)} for at_y in range(4)]

    def react(at_y, events):
        used.update(marks[at_y])
        for kind, *where in events:
            if kind == RELAY:
                relay(at_y, *where)
            elif kind == SUM:
                for piece_kind in (UPPER, LOWER):
                    for part in range(2):
                        key = (piece_kind, *where, part)
                        if key not in waited[at_y]:
                            wait_piece(at_y, piece_kind, slab_at(*where), part)
                        waited[at_y].add(key)
            else:
                wait_piece(at_y, kind, slab_at(*where[:2]), where[2])
                waited[at_y].add((kind, *where))
                go_on(at_y, kind, *where)
        marks[at_y] = dict(used)

    for n in range(8):
        slab = my_slab * 0
        for at_y in range(4):
            events = steps(at_y)[n]
            pl.when(y == at_y)(functools.partial(react, at_y, events))
            slab = jnp.where(y == at_y, slab_at(*events[-1][1:]), slab)
        accumulate(slab)

    order = (2, 1, 3, 0)

    def rows_of(to_y, of_core):
        return pl.ds(pl.multiple_of((to_y // 2) * (2 * rows) + of_core * rows, rows), rows)

    sums = []
    for n, dy in enumerate(order):
        to_y = (y + dy) % 4
        when = (x < 3) | (to_y < 2)
        copy = remote(
            acc.at[to_y % 2, rows_of(to_y, 1 - core)], other.at[n], send_sum.at[n], recv_sum.at[n], device(0, 0, 1))
        pl.when(when)(copy.start)
        sums.append((when, copy))

    def out_counts(of_y):
        return ((of_y < 3, main), (of_y == 3, lower))

    outs = []
    for n, dy in enumerate(order):
        to_y = (y + dy) % 4
        when, copy = sums[n]

        @pl.when(when)
        def _(n=n, dy=dy, to_y=to_y, copy=copy):
            copy.wait_recv()
            keep = rows_of(to_y, core)
            value = weight[keep] * (acc[to_y % 2, keep] + other[n])
            if dy == 0:
                for size_when, count in out_counts(y):
                    @pl.when(size_when)
                    def _(count=count):
                        out_ref[0, :, pl.ds(d_start, count)] = value[:, :count]
            else:
                largest = jnp.max(jnp.abs(value), axis=0, keepdims=True)
                unit = jnp.where(largest > 0.0, 1.0 / largest, 0.0)
                coded[n] = jnp.round(value * unit * 32767.0).astype(jnp.int32).astype(jnp.int16)
                gain[n] = largest

        if dy != 0:
            copies = [(when, remote(gain.at[n], got_gain.at[y], send_out.at[1, n], recv_out.at[1, y], device(0, dy)))]
            for size_when, count in out_counts(y):
                copies.append((when & size_when, remote(
                    coded.at[n, :, pl.ds(0, count)], got.at[:, pl.ds(d_start, count)],
                    send_out.at[0, n], recv_out.at[0, y], device(0, dy))))
            for start_when, out in copies:
                pl.when(start_when)(out.start)
            outs += copies

    have_out = (x < 3) | (half == 0)
    for dy in (1, 3, 2):
        from_y = (y + dy) % 4

        @pl.when(have_out)
        def _(from_y=from_y):
            remote(got_gain.at[from_y], got_gain.at[from_y], send_out.at[1, 0], recv_out.at[1, from_y], device(1, 0)).wait_recv()

        for size_when, count in out_counts(from_y):
            @pl.when(have_out & size_when)
            def _(from_y=from_y, count=count):
                columns = pl.ds(pl.multiple_of(from_y * main, LANES), count)
                here = got.at[:, columns]
                remote(here, here, send_out.at[0, 0], recv_out.at[0, from_y], device(1, 0)).wait_recv()
                value = got[:, columns].astype(jnp.int32).astype(jnp.float32) * (1.0 / 32767.0)
                out_ref[0, :, columns] = value * got_gain[from_y][:, :count]

    for at_y in range(4):
        @pl.when(y == at_y)
        def _(at_y=at_y):
            for make in pending[at_y]:
                for when, copy in make():
                    pl.when(when)(copy.wait_send)
    for when, copy in sums + outs:
        pl.when(when)(copy.wait_send)


def per_device(s_real, s_imag, chan_l, counts, jlevel, allowed, recoup):
    rows, width = s_real.shape[1:]
    live, upper, main, extra, lower = plan(rows, width)
    vmem = pl.BlockSpec(memory_space=pltpu.VMEM)
    dma = pltpu.SemaphoreType.DMA
    return pl.pallas_call(
        functools.partial(kernel, rows, width),
        grid=(1,),
        out_shape=jax.ShapeDtypeStruct((1, rows, width), jnp.float32),
        in_specs=[pl.BlockSpec(memory_space=pltpu.HBM)] * 2 + [vmem] * 5,
        out_specs=vmem,
        scratch_shapes=[
            pltpu.VMEM((14 * rows, upper), jnp.bfloat16),
            pltpu.VMEM((14 * rows, lower), jnp.bfloat16),
            pltpu.VMEM((2 * rows, lower), jnp.bfloat16),
            pltpu.VMEM((2, 2 * rows, lower), jnp.bfloat16),
            pltpu.VMEM((2, upper, lower), jnp.float32),
            pltpu.VMEM((4, rows, lower), jnp.float32),
            pltpu.VMEM((4, rows, lower), jnp.int16),
            pltpu.VMEM((rows, live), jnp.int16),
            pltpu.VMEM((4, 1, lower), jnp.float32),
            pltpu.VMEM((4, 1, lower), jnp.float32),
            pltpu.VMEM((upper, lower), jnp.float32),
            pltpu.VMEM((1, width + 2 * LANES), jnp.int32),
            pltpu.VMEM((1, width + 2 * LANES), jnp.int32),
            pltpu.VMEM((8, width + 2 * LANES), jnp.int32),
            dma((40,)), dma((7, 2)), dma((40,)), dma((7, 2)), dma((2,)),
            dma((4,)), dma((4,)), dma((2, 4)), dma((2, 4)), dma((8,)),
        ],
        compiler_params=pltpu.CompilerParams(
            collective_id=0, has_side_effects=True, vmem_limit_bytes=61 << 20),
        cost_estimate=pl.CostEstimate(
            flops=16 * 7 * rows * upper * lower, bytes_accessed=8 * rows * width, transcendentals=0),
    )(s_real, s_imag, chan_l, counts[:, None], jlevel[:, None], allowed, recoup)


def solution(mesh):
    placed = (
        P("jpair", "row", None),
        P("jpair", "row", None),
        P("jpair", None),
        P("jpair"),
        P("jpair"),
        P(),
        P(),
    )
    return jax.shard_map(
        per_device, mesh=mesh, in_specs=placed, out_specs=P("jpair", "row", None), check_vma=False
    )
```

```python
import functools

import jax
import jax.numpy as jnp
from jax import lax
from jax.experimental import pallas as pl
from jax.experimental.pallas import tpu as pltpu
from jax.sharding import PartitionSpec as P

MESH = pl.DeviceIdType.MESH
LANES = 128
RELAY, UPPER, LOWER, SUM = range(4)
ORDER = (
    (
        (RELAY, 0), (RELAY, 1), (UPPER, 1, 0, 0), (UPPER, 3, 0, 0), (LOWER, 0, 1, 0), (LOWER, 0, 0, 0),
        (UPPER, 1, 0, 1), (LOWER, 0, 1, 1), (UPPER, 3, 0, 1), (LOWER, 0, 0, 1), (SUM, 0, 0), (LOWER, 1, 1, 0),
        (SUM, 0, 1), (UPPER, 2, 0, 0), (LOWER, 3, 1, 0), (LOWER, 1, 0, 0), (LOWER, 3, 0, 0), (UPPER, 2, 0, 1),
        (LOWER, 1, 1, 1), (LOWER, 3, 1, 1), (SUM, 1, 1), (LOWER, 1, 0, 1), (LOWER, 3, 0, 1), (SUM, 3, 1),
        (SUM, 1, 0), (SUM, 3, 0), (SUM, 2, 0), (SUM, 2, 1),
    ),
    (
        (LOWER, 1, 0, 0), (LOWER, 3, 0, 0), (UPPER, 0, 0, 0), (UPPER, 0, 1, 1), (LOWER, 1, 0, 1), (LOWER, 3, 0, 1),
        (LOWER, 0, 1, 0), (LOWER, 0, 1, 1), (UPPER, 1, 0, 0), (SUM, 0, 1), (LOWER, 3, 1, 0), (LOWER, 1, 1, 0),
        (UPPER, 1, 1, 1), (UPPER, 3, 0, 0), (LOWER, 3, 1, 1), (LOWER, 1, 1, 1), (SUM, 1, 1), (SUM, 1, 0),
        (UPPER, 3, 1, 1), (SUM, 3, 0), (UPPER, 2, 0, 0), (SUM, 3, 1), (UPPER, 2, 1, 1), (SUM, 0, 0), (SUM, 2, 0),
        (SUM, 2, 1),
    ),
    (
        (RELAY, 1), (RELAY, 0), (UPPER, 1, 0, 0), (UPPER, 3, 0, 0), (LOWER, 0, 0, 0), (LOWER, 0, 1, 0),
        (UPPER, 1, 0, 1), (UPPER, 3, 0, 1), (LOWER, 0, 0, 1), (LOWER, 0, 1, 1), (SUM, 0, 0), (UPPER, 0, 1, 1),
        (UPPER, 0, 1, 0), (LOWER, 1, 0, 0), (SUM, 0, 1), (UPPER, 2, 0, 0), (LOWER, 1, 1, 0), (LOWER, 3, 0, 0),
        (LOWER, 1, 0, 1), (LOWER, 3, 1, 0), (SUM, 1, 0), (UPPER, 2, 0, 1), (LOWER, 1, 1, 1), (LOWER, 3, 0, 1),
        (SUM, 1, 1), (SUM, 3, 0), (LOWER, 3, 1, 1), (SUM, 3, 1), (SUM, 2, 0), (SUM, 2, 1),
    ),
    (
        (UPPER, 0, 0, 0), (UPPER, 0, 1, 1), (LOWER, 1, 0, 0), (LOWER, 3, 0, 0), (LOWER, 1, 0, 1), (LOWER, 3, 0, 1),
        (LOWER, 0, 1, 1), (SUM, 0, 0), (LOWER, 0, 1, 0), (UPPER, 1, 1, 1), (UPPER, 1, 0, 0), (LOWER, 3, 1, 1),
        (LOWER, 1, 1, 1), (UPPER, 3, 0, 0), (LOWER, 3, 1, 0), (UPPER, 3, 1, 1), (LOWER, 1, 1, 0), (SUM, 1, 1),
        (SUM, 1, 0), (SUM, 3, 1), (UPPER, 2, 0, 0), (UPPER, 2, 1, 1), (SUM, 3, 0), (SUM, 0, 1), (SUM, 2, 0),
        (SUM, 2, 1),
    ),
)


def plan(rows, width):
    live = 14 * rows
    upper = 4 * rows
    main = live // LANES // 4 * LANES
    extra = live - 4 * main
    return live, upper, main, extra, main + extra


def kernel(
    rows, width, re_ref, im_ref, chan_ref, count_ref, level_ref, allowed_ref, recoup_ref, got, got_unit,
    up, low, transit, swapped, acc, other, coded, unit, weight, zeros, mine, theirs, labels,
    send_up, recv_up, send_low, recv_low, recv_transit, send_sum, recv_sum, send_out, recv_out, local_sem,
):
    live, upper, main, extra, lower = plan(rows, width)
    j, r = lax.axis_index("jpair"), lax.axis_index("row")
    pair, parity = j // 2, j % 2
    x, half, core = r // 4, (r // 2) % 2, r % 2
    y = 2 * half + parity
    is_upper, is_lower = parity == 0, parity == 1
    source = (re_ref, im_ref)

    def device(dx, dy, dcore=0):
        to_x, to_y = (x + dx) % 4, (y + dy) % 4
        return (2 * pair + to_y % 2, 4 * to_x + 2 * (to_y // 2) + (core + dcore) % 2)

    def remote(src, dst, send, recv, where):
        return pltpu.make_async_remote_copy(
            src_ref=src, dst_ref=dst, send_sem=send, recv_sem=recv, device_id=where, device_id_type=MESH
        )

    barrier = pltpu.get_barrier_semaphore()
    greeted = [(1, 0, 0), (3, 0, 0), (2, 0, 0), (0, 1, 0), (0, 3, 0), (0, 2, 0), (0, 0, 1)]
    for offset in greeted:
        pl.semaphore_signal(barrier, inc=1, device_id=device(*offset), device_id_type=MESH)
    pl.semaphore_wait(barrier, len(greeted))

    def slab_at(dx, dhalf):
        return 2 * ((x + dx) % 4) + (half + dhalf) % 2

    def piece(buffer, slab, part, count):
        return buffer.at[pl.ds(pl.multiple_of(slab * (2 * rows) + part * rows, rows), rows), pl.ds(0, count)]

    my_slab = slab_at(0, 0)
    have_rows = my_slab < 7
    up_from, low_from = is_upper & have_rows, is_lower & have_rows

    mine[:, :width] = chan_ref[...]
    mine[:, width:width + LANES] = jnp.broadcast_to(count_ref[...], (1, LANES))
    mine[:, width + LANES:] = jnp.broadcast_to(level_ref[...], (1, LANES))
    meta_copy = remote(mine, theirs, local_sem.at[0], local_sem.at[1], device(0, 1 - 2 * parity))
    meta_copy.start()

    def low_count(to_y):
        return lower if to_y % 4 == 3 else main

    def up_columns(part, to_x):
        return lambda count: source[part].at[0, :, pl.ds(pl.multiple_of(to_x * upper, LANES), count)]

    def low_columns(part, to_y, count):
        return source[part].at[0, :, pl.ds(pl.multiple_of(to_y * main, LANES), count)]

    pending = [[] for _ in range(4)]
    used = {"up": 0, "low": 0}

    def send(at_y, make):
        for when, copy in make():
            pl.when(when)(copy.start)
        pending[at_y].append(make)

    def send_up_piece(at_y, when, src, part, dx, dhalf, to):
        n = used["up"]
        used["up"] += 1

        def make():
            slab = slab_at(dx, dhalf)
            ok = (slab < 7) if when is None else (slab < 7) & when()
            to_x = (x + to[0]) % 4
            return [
                (ok & size_when, remote(
                    src(slab, count), piece(up, slab, part, count), send_up.at[n], recv_up.at[slab, part], device(*to)))
                for size_when, count in ((to_x < 3, upper), (to_x == 3, 2 * rows))]

        send(at_y, make)

    def send_low_piece(at_y, src, part, dx, dhalf, to, count, when=None, passing=False):
        n = used["low"]
        used["low"] += 1

        def make():
            slab = slab_at(dx, dhalf)
            if passing:
                dst, recv = transit.at[pl.ds(part * rows, rows), pl.ds(0, count)], recv_transit.at[part]
            else:
                dst, recv = piece(low, slab, part, count), recv_low.at[slab, part]
            ok = (slab < 7) if when is None else (slab < 7) & when()
            return [(ok, remote(src(slab), dst, send_low.at[n], recv, device(*to)))]

        send(at_y, make)

    def begin(at_y):
        used["up"] = used["low"] = 0
        if at_y % 2 == 0:
            for part, dy in ((0, 1), (1, 3), (0, 3), (1, 1)):
                when = (lambda: x == 3) if at_y == 0 and dy != 1 + 2 * part else None
                send_up_piece(at_y, when, lambda slab, count, part=part: up_columns(part, x)(count), part, 0, 0, (0, dy))
            for dx in (1, 3, 2):
                for part in range(2):
                    send_up_piece(
                        at_y, None, lambda slab, count, part=part, dx=dx: up_columns(part, (x + dx) % 4)(count),
                        part, 0, 0, (dx, 0))
        else:
            to = [(0, part, 1 + 2 * part, at_y + 2) for part in range(2)]
            to += [(0, part, dy, at_y + dy) for part in range(2) for dy in (1, 3)]
            to += [(dx, part, 0, at_y) for part in range(2) for dx in (1, 3)]
            for n, (dx, part, dy, to_y) in enumerate(to):
                count = low_count(to_y)
                send_low_piece(
                    at_y, lambda slab, part=part, to_y=to_y, count=count: low_columns(part, to_y % 4, count),
                    part, 0, 0, (dx, dy), count, passing=n < 2)
        marks.append(dict(used))

    marks = []
    for at_y in range(4):
        pl.when(y == at_y)(functools.partial(begin, at_y))

    own = []
    for part in range(2):
        own.append((up_from, pltpu.make_async_copy(
            up_columns(part, x)(upper), piece(up, my_slab, part, upper), local_sem.at[2 + part])))
        own.append((low_from, pltpu.make_async_copy(
            low_columns(part, y, lower), piece(low, my_slab, part, lower), local_sem.at[2 + part])))
    for when, copy in own:
        pl.when(when)(copy.start)

    zeros[...] = jnp.zeros_like(zeros)
    blank = []
    for when, columns in ((my_slab < 7, pl.ds(live, width - live)), (my_slab == 7, pl.ds(0, width))):
        blank.append((when, pltpu.make_async_copy(zeros.at[:, columns], got_unit.at[:, columns], local_sem.at[4])))
    for when, copy in blank:
        pl.when(when)(copy.start)
    acc[...] = jnp.zeros_like(acc)

    meta_copy.wait()
    first = jnp.where(is_upper, mine[...], theirs[...])
    second = jnp.where(is_upper, theirs[...], mine[...])
    upper_count, lower_count = first[:, width:width + 1], second[:, width:width + 1]
    upper_deg = (2 * first[:, width + LANES:width + LANES + 1] + 1).astype(jnp.float32)
    lower_deg = (2 * second[:, width + LANES:width + LANES + 1] + 1).astype(jnp.float32)
    factor = 2.0 * lower_deg / (upper_deg + lower_deg)
    labels[0:1, :] = first
    labels[1:2, :] = second
    table = recoup_ref[...] * allowed_ref[...].astype(jnp.float32)
    levels = table.shape[0]
    c_start = pl.multiple_of(x * upper, LANES)
    d_start = pl.multiple_of(y * main, LANES)
    c_labels = labels[0:1, pl.ds(c_start, upper)]
    d_labels = labels[1:2, pl.ds(d_start, lower)]
    c_open = c_start + lax.broadcasted_iota(jnp.int32, (1, upper), 1) < upper_count
    d_open = d_start + lax.broadcasted_iota(jnp.int32, (1, lower), 1) < lower_count
    c_labels = jnp.where(c_open, c_labels, -1)
    d_labels = jnp.where(d_open, d_labels, -1)
    c_hot = (lax.broadcasted_iota(jnp.int32, (levels, upper), 0) == c_labels).astype(jnp.float32)
    d_hot = (lax.broadcasted_iota(jnp.int32, (levels, lower), 0) == d_labels).astype(jnp.float32)
    picked = factor * jnp.dot(
        table, d_hot, precision=lax.Precision.HIGHEST, preferred_element_type=jnp.float32)
    weight[...] = lax.dot_general(
        c_hot, picked, (((0,), (0,)), ((), ())),
        precision=lax.Precision.HIGHEST, preferred_element_type=jnp.float32)
    least = jnp.minimum(upper_count, lower_count)
    for when, copy in own:
        pl.when(when)(copy.wait)

    tile = min(256, upper)

    def accumulate(slab):
        @pl.when(slab < 7)
        def _():
            row = pl.multiple_of(slab * 2 * rows, rows)
            first_row = (slab // 2) * (4 * rows) + (slab % 2) * (2 * rows) + core * rows
            row_ids = first_row + lax.broadcasted_iota(jnp.int32, (rows, lower), 0)
            keep = (row_ids < least).astype(jnp.float32).astype(jnp.bfloat16)
            low_re = low[pl.ds(row, rows)] * keep
            low_im = low[pl.ds(pl.multiple_of(row + rows, rows), rows)] * keep
            swapped[0, :rows] = low_re
            swapped[0, rows:] = low_im
            swapped[1, :rows] = low_im
            swapped[1, rows:] = -low_re

            @pl.loop(0, upper // tile)
            def _(n):
                start = pl.multiple_of(n * tile, tile)
                left = up[pl.ds(row, 2 * rows), pl.ds(start, tile)]
                for part in range(2):
                    acc[part, pl.ds(start, tile)] += lax.dot_general(
                        left, swapped[part], (((0,), (0,)), ((), ())), preferred_element_type=jnp.float32)

    def wait_piece(at_y, kind, slab, part):
        if kind == UPPER:
            for size_when, count in ((x < 3, upper), (x == 3, 2 * rows)):
                here = piece(up, slab, part, count)
                pl.when((slab < 7) & size_when)(
                    remote(here, here, send_up.at[0], recv_up.at[slab, part], device(1, 0)).wait_recv)
        else:
            here = piece(low, slab, part, low_count(at_y))
            pl.when(slab < 7)(remote(here, here, send_low.at[0], recv_low.at[slab, part], device(1, 0)).wait_recv)

    def go_on(at_y, kind, dx, dhalf, part):
        if kind == LOWER:
            usual = part == (0 if dx == 3 else 1)
            if dx == 0:
                when = None
            elif usual:
                when = None if dhalf == 0 else (lambda: x != 1)
            else:
                when = (lambda: x == 3) if dhalf == 1 else (lambda: x < 0)
            count = low_count(at_y)
            for to_dx in ((1, 3) if dx == 0 else (4 - dx,)):
                send_low_piece(
                    at_y, lambda slab: piece(low, slab, part, count), part, dx, dhalf, (to_dx, 0), count, when)
            return
        when = None
        if at_y % 2 == 1:
            hops = [(part, 1 + 2 * part)]
        elif dhalf == 1:
            hops = [(part, 1 + 2 * part)]
            when = lambda: x < 3
        elif part == 0:
            hops = [(0, 1)]
        else:
            hops = [(1, 3), (0, 3), (1, 1)]
        for of_part, dy in hops:
            send_up_piece(
                at_y, when, lambda slab, count, of_part=of_part: piece(up, slab, of_part, count),
                of_part, dx, dhalf, (0, dy))

    def relay(at_y, part):
        dy = 1 + 2 * part
        count = low_count(at_y + dy)
        here = transit.at[pl.ds(part * rows, rows), pl.ds(0, count)]
        pl.when(slab_at(0, 1 - part) < 7)(
            remote(here, here, send_low.at[0], recv_transit.at[part], device(1, 0)).wait_recv)
        send_low_piece(at_y, lambda slab: here, part, 0, 1 - part, (0, dy), count)

    def steps(at_y):
        cut = [[]]
        for event in ORDER[at_y]:
            cut[-1].append(event)
            if event[0] == SUM:
                cut.append([])
        return cut

    waited = [{(UPPER if at_y % 2 == 0 else LOWER, 0, 0, part) for part in range(2)} for at_y in range(4)]

    def react(at_y, events):
        used.update(marks[at_y])
        for kind, *where in events:
            if kind == RELAY:
                relay(at_y, *where)
            elif kind == SUM:
                for piece_kind in (UPPER, LOWER):
                    for part in range(2):
                        key = (piece_kind, *where, part)
                        if key not in waited[at_y]:
                            wait_piece(at_y, piece_kind, slab_at(*where), part)
                        waited[at_y].add(key)
            else:
                wait_piece(at_y, kind, slab_at(*where[:2]), where[2])
                waited[at_y].add((kind, *where))
                go_on(at_y, kind, *where)
        marks[at_y] = dict(used)

    for n in range(8):
        slab = my_slab * 0
        for at_y in range(4):
            events = steps(at_y)[n]
            pl.when(y == at_y)(functools.partial(react, at_y, events))
            slab = jnp.where(y == at_y, slab_at(*events[-1][1:]), slab)
        accumulate(slab)

    order = (2, 1, 3, 0)

    def rows_of(to_y, of_core):
        return pl.ds(pl.multiple_of((to_y // 2) * (2 * rows) + of_core * rows, rows), rows)

    sums = []
    for n, dy in enumerate(order):
        to_y = (y + dy) % 4
        when = (x < 3) | (to_y < 2)
        copy = remote(
            acc.at[to_y % 2, rows_of(to_y, 1 - core)], other.at[n], send_sum.at[n], recv_sum.at[n], device(0, 0, 1))
        pl.when(when)(copy.start)
        sums.append((when, copy))

    def out_counts(of_y):
        return ((of_y < 3, main), (of_y == 3, lower))

    outs, kept = [], []
    for n, dy in enumerate(order):
        to_y = (y + dy) % 4
        when, copy = sums[n]

        @pl.when(when)
        def _(n=n, to_y=to_y, copy=copy):
            copy.wait_recv()
            keep = rows_of(to_y, core)
            value = weight[keep] * (acc[to_y % 2, keep] + other[n])
            largest = jnp.max(jnp.abs(value), axis=0, keepdims=True)
            over = jnp.where(largest > 0.0, 1.0 / largest, 0.0)
            coded[n] = jnp.round(value * over * 32767.0).astype(jnp.int32).astype(jnp.int16)
            unit[n] = largest

        for size_when, count in out_counts(y):
            here = when & size_when
            columns = pl.ds(d_start, count)
            pairs = (
                (unit.at[n, :, pl.ds(0, count)], got_unit.at[:, columns], 1),
                (coded.at[n, :, pl.ds(0, count)], got.at[:, columns], 0),
            )
            for src, dst, m in pairs:
                if dy == 0:
                    kept.append((here, pltpu.make_async_copy(src, dst, local_sem.at[5 + m])))
                    pl.when(here)(kept[-1][1].start)
                else:
                    outs.append((here, remote(src, dst, send_out.at[m, n], recv_out.at[m, y], device(0, dy))))
                    pl.when(here)(outs[-1][1].start)

    have_out = (x < 3) | (half == 0)
    for dy in (1, 3, 2):
        from_y = (y + dy) % 4
        for size_when, count in out_counts(from_y):
            @pl.when(have_out & size_when)
            def _(from_y=from_y, count=count):
                columns = pl.ds(pl.multiple_of(from_y * main, LANES), count)
                for m, here in ((1, got_unit.at[:, columns]), (0, got.at[:, columns])):
                    remote(here, here, send_out.at[m, 0], recv_out.at[m, from_y], device(1, 0)).wait_recv()

    for when, copy in blank + kept:
        pl.when(when)(copy.wait)
    for at_y in range(4):
        @pl.when(y == at_y)
        def _(at_y=at_y):
            for make in pending[at_y]:
                for when, copy in make():
                    pl.when(when)(copy.wait_send)
    for when, copy in sums + outs:
        pl.when(when)(copy.wait_send)


def per_device(s_real, s_imag, chan_l, counts, jlevel, allowed, recoup):
    rows, width = s_real.shape[1:]
    live, upper, main, extra, lower = plan(rows, width)
    vmem, anywhere = pl.BlockSpec(memory_space=pltpu.VMEM), pl.BlockSpec(memory_space=pl.ANY)
    dma = pltpu.SemaphoreType.DMA
    got, unit = pl.pallas_call(
        functools.partial(kernel, rows, width),
        grid=(1,),
        out_shape=(jax.ShapeDtypeStruct((rows, width), jnp.int16), jax.ShapeDtypeStruct((1, width), jnp.float32)),
        in_specs=[anywhere] * 2 + [vmem] * 5,
        out_specs=(anywhere, anywhere),
        scratch_shapes=[
            pltpu.VMEM((14 * rows, upper), jnp.bfloat16),
            pltpu.VMEM((14 * rows, lower), jnp.bfloat16),
            pltpu.VMEM((2 * rows, lower), jnp.bfloat16),
            pltpu.VMEM((2, 2 * rows, lower), jnp.bfloat16),
            pltpu.VMEM((2, upper, lower), jnp.float32),
            pltpu.VMEM((4, rows, lower), jnp.float32),
            pltpu.VMEM((4, rows, lower), jnp.int16),
            pltpu.VMEM((4, 1, lower), jnp.float32),
            pltpu.VMEM((upper, lower), jnp.float32),
            pltpu.VMEM((1, width), jnp.float32),
            pltpu.VMEM((1, width + 2 * LANES), jnp.int32),
            pltpu.VMEM((1, width + 2 * LANES), jnp.int32),
            pltpu.VMEM((8, width + 2 * LANES), jnp.int32),
            dma((40,)), dma((7, 2)), dma((40,)), dma((7, 2)), dma((2,)),
            dma((4,)), dma((4,)), dma((2, 4)), dma((2, 4)), dma((8,)),
        ],
        compiler_params=pltpu.CompilerParams(
            collective_id=0, has_side_effects=True, vmem_limit_bytes=61 << 20),
        cost_estimate=pl.CostEstimate(
            flops=16 * 7 * rows * upper * lower, bytes_accessed=8 * rows * width, transcendentals=0),
    )(s_real, s_imag, chan_l, counts[:, None], jlevel[:, None], allowed, recoup)
    share = jnp.maximum(got.astype(jnp.float32) * (1.0 / 32767.0), -1.0)
    return (share * unit)[None]


def solution(mesh):
    placed = (
        P("jpair", "row", None),
        P("jpair", "row", None),
        P("jpair", None),
        P("jpair"),
        P("jpair"),
        P(),
        P(),
    )
    return jax.shard_map(
        per_device, mesh=mesh, in_specs=placed, out_specs=P("jpair", "row", None), check_vma=False
    )
```

```python
import functools

import jax
import jax.numpy as jnp
from jax import lax
from jax.experimental import pallas as pl
from jax.experimental.pallas import tpu as pltpu
from jax.sharding import PartitionSpec as P

MESH = pl.DeviceIdType.MESH
LANES = 128
RELAY, UPPER, LOWER, SUM = range(4)
ORDER = (
    (
        (RELAY, 0), (RELAY, 1), (UPPER, 1, 0, 0), (UPPER, 3, 0, 0), (LOWER, 0, 1, 0), (LOWER, 0, 0, 0),
        (UPPER, 1, 0, 1), (LOWER, 0, 1, 1), (UPPER, 3, 0, 1), (LOWER, 0, 0, 1), (SUM, 0, 0), (LOWER, 1, 1, 0),
        (SUM, 0, 1), (UPPER, 2, 0, 0), (LOWER, 3, 1, 0), (LOWER, 1, 0, 0), (LOWER, 3, 0, 0), (UPPER, 2, 0, 1),
        (LOWER, 1, 1, 1), (LOWER, 3, 1, 1), (SUM, 1, 1), (LOWER, 1, 0, 1), (LOWER, 3, 0, 1), (SUM, 3, 1),
        (SUM, 1, 0), (SUM, 3, 0), (SUM, 2, 0), (SUM, 2, 1),
    ),
    (
        (LOWER, 1, 0, 0), (LOWER, 3, 0, 0), (UPPER, 0, 0, 0), (UPPER, 0, 1, 1), (LOWER, 1, 0, 1), (LOWER, 3, 0, 1),
        (LOWER, 0, 1, 0), (LOWER, 0, 1, 1), (UPPER, 1, 0, 0), (SUM, 0, 1), (LOWER, 3, 1, 0), (LOWER, 1, 1, 0),
        (UPPER, 1, 1, 1), (UPPER, 3, 0, 0), (LOWER, 3, 1, 1), (LOWER, 1, 1, 1), (SUM, 1, 1), (SUM, 1, 0),
        (UPPER, 3, 1, 1), (SUM, 3, 0), (UPPER, 2, 0, 0), (SUM, 3, 1), (UPPER, 2, 1, 1), (SUM, 0, 0), (SUM, 2, 0),
        (SUM, 2, 1),
    ),
    (
        (RELAY, 1), (RELAY, 0), (UPPER, 1, 0, 0), (UPPER, 3, 0, 0), (LOWER, 0, 0, 0), (LOWER, 0, 1, 0),
        (UPPER, 1, 0, 1), (UPPER, 3, 0, 1), (LOWER, 0, 0, 1), (LOWER, 0, 1, 1), (SUM, 0, 0), (UPPER, 0, 1, 1),
        (UPPER, 0, 1, 0), (LOWER, 1, 0, 0), (SUM, 0, 1), (UPPER, 2, 0, 0), (LOWER, 1, 1, 0), (LOWER, 3, 0, 0),
        (LOWER, 1, 0, 1), (LOWER, 3, 1, 0), (SUM, 1, 0), (UPPER, 2, 0, 1), (LOWER, 1, 1, 1), (LOWER, 3, 0, 1),
        (SUM, 1, 1), (SUM, 3, 0), (LOWER, 3, 1, 1), (SUM, 3, 1), (SUM, 2, 0), (SUM, 2, 1),
    ),
    (
        (UPPER, 0, 0, 0), (UPPER, 0, 1, 1), (LOWER, 1, 0, 0), (LOWER, 3, 0, 0), (LOWER, 1, 0, 1), (LOWER, 3, 0, 1),
        (LOWER, 0, 1, 1), (SUM, 0, 0), (LOWER, 0, 1, 0), (UPPER, 1, 1, 1), (UPPER, 1, 0, 0), (LOWER, 3, 1, 1),
        (LOWER, 1, 1, 1), (UPPER, 3, 0, 0), (LOWER, 3, 1, 0), (UPPER, 3, 1, 1), (LOWER, 1, 1, 0), (SUM, 1, 1),
        (SUM, 1, 0), (SUM, 3, 1), (UPPER, 2, 0, 0), (UPPER, 2, 1, 1), (SUM, 3, 0), (SUM, 0, 1), (SUM, 2, 0),
        (SUM, 2, 1),
    ),
)


def plan(rows, width):
    live = 14 * rows
    upper = 4 * rows
    main = live // LANES // 4 * LANES
    extra = live - 4 * main
    return live, upper, main, extra, main + extra


def kernel(
    rows, width, re_ref, im_ref, chan_ref, count_ref, level_ref, allowed_ref, recoup_ref, got, got_unit,
    chan, allowed, recoup,
    up, low, transit, swapped, acc, other, coded, unit, weight, zeros, mine, theirs, labels,
    send_up, recv_up, send_low, recv_low, recv_transit, send_sum, recv_sum, send_out, recv_out, local_sem,
):
    live, upper, main, extra, lower = plan(rows, width)
    j, r = lax.axis_index("jpair"), lax.axis_index("row")
    pair, parity = j // 2, j % 2
    x, half, core = r // 4, (r // 2) % 2, r % 2
    y = 2 * half + parity
    is_upper, is_lower = parity == 0, parity == 1
    source = (re_ref, im_ref)

    def device(dx, dy, dcore=0):
        to_x, to_y = (x + dx) % 4, (y + dy) % 4
        return (2 * pair + to_y % 2, 4 * to_x + 2 * (to_y // 2) + (core + dcore) % 2)

    def remote(src, dst, send, recv, where):
        return pltpu.make_async_remote_copy(
            src_ref=src, dst_ref=dst, send_sem=send, recv_sem=recv, device_id=where, device_id_type=MESH
        )

    small = [
        pltpu.make_async_copy(src, dst, local_sem.at[8 + n])
        for n, (src, dst) in enumerate(((chan_ref, chan), (allowed_ref, allowed), (recoup_ref, recoup)))]
    for copy in small:
        copy.start()
    barrier = pltpu.get_barrier_semaphore()
    greeted = [(1, 0, 0), (3, 0, 0), (2, 0, 0), (0, 1, 0), (0, 3, 0), (0, 2, 0), (0, 0, 1)]
    for offset in greeted:
        pl.semaphore_signal(barrier, inc=1, device_id=device(*offset), device_id_type=MESH)
    pl.semaphore_wait(barrier, len(greeted))

    def slab_at(dx, dhalf):
        return 2 * ((x + dx) % 4) + (half + dhalf) % 2

    def piece(buffer, slab, part, count):
        return buffer.at[pl.ds(pl.multiple_of(slab * (2 * rows) + part * rows, rows), rows), pl.ds(0, count)]

    my_slab = slab_at(0, 0)
    have_rows = my_slab < 7
    up_from, low_from = is_upper & have_rows, is_lower & have_rows

    for copy in small:
        copy.wait()
    mine[:, :width] = chan[...]
    mine[:, width:width + LANES] = jnp.broadcast_to(count_ref[...], (1, LANES))
    mine[:, width + LANES:] = jnp.broadcast_to(level_ref[...], (1, LANES))
    meta_copy = remote(mine, theirs, local_sem.at[0], local_sem.at[1], device(0, 1 - 2 * parity))
    meta_copy.start()

    def low_count(to_y):
        return lower if to_y % 4 == 3 else main

    def up_columns(part, to_x):
        return lambda count: source[part].at[0, :, pl.ds(pl.multiple_of(to_x * upper, LANES), count)]

    def low_columns(part, to_y, count):
        return source[part].at[0, :, pl.ds(pl.multiple_of(to_y * main, LANES), count)]

    pending = [[] for _ in range(4)]
    used = {"up": 0, "low": 0}

    def send(at_y, make):
        for when, copy in make():
            pl.when(when)(copy.start)
        pending[at_y].append(make)

    def send_up_piece(at_y, when, src, part, dx, dhalf, to):
        n = used["up"]
        used["up"] += 1

        def make():
            slab = slab_at(dx, dhalf)
            ok = (slab < 7) if when is None else (slab < 7) & when()
            to_x = (x + to[0]) % 4
            return [
                (ok & size_when, remote(
                    src(slab, count), piece(up, slab, part, count), send_up.at[n], recv_up.at[slab, part], device(*to)))
                for size_when, count in ((to_x < 3, upper), (to_x == 3, 2 * rows))]

        send(at_y, make)

    def send_low_piece(at_y, src, part, dx, dhalf, to, count, when=None, passing=False):
        n = used["low"]
        used["low"] += 1

        def make():
            slab = slab_at(dx, dhalf)
            if passing:
                dst, recv = transit.at[pl.ds(part * rows, rows), pl.ds(0, count)], recv_transit.at[part]
            else:
                dst, recv = piece(low, slab, part, count), recv_low.at[slab, part]
            ok = (slab < 7) if when is None else (slab < 7) & when()
            return [(ok, remote(src(slab), dst, send_low.at[n], recv, device(*to)))]

        send(at_y, make)

    def begin(at_y):
        used["up"] = used["low"] = 0
        if at_y % 2 == 0:
            for part, dy in ((0, 1), (1, 3), (0, 3), (1, 1)):
                when = (lambda: x == 3) if at_y == 0 and dy != 1 + 2 * part else None
                send_up_piece(at_y, when, lambda slab, count, part=part: up_columns(part, x)(count), part, 0, 0, (0, dy))
            for dx in (1, 3, 2):
                for part in range(2):
                    send_up_piece(
                        at_y, None, lambda slab, count, part=part, dx=dx: up_columns(part, (x + dx) % 4)(count),
                        part, 0, 0, (dx, 0))
        else:
            to = [(0, part, 1 + 2 * part, at_y + 2) for part in range(2)]
            to += [(0, part, dy, at_y + dy) for part in range(2) for dy in (1, 3)]
            to += [(dx, part, 0, at_y) for part in range(2) for dx in (1, 3)]
            for n, (dx, part, dy, to_y) in enumerate(to):
                count = low_count(to_y)
                send_low_piece(
                    at_y, lambda slab, part=part, to_y=to_y, count=count: low_columns(part, to_y % 4, count),
                    part, 0, 0, (dx, dy), count, passing=n < 2)
        marks.append(dict(used))

    marks = []
    for at_y in range(4):
        pl.when(y == at_y)(functools.partial(begin, at_y))

    own = []
    for part in range(2):
        own.append((up_from, pltpu.make_async_copy(
            up_columns(part, x)(upper), piece(up, my_slab, part, upper), local_sem.at[2 + part])))
        own.append((low_from, pltpu.make_async_copy(
            low_columns(part, y, lower), piece(low, my_slab, part, lower), local_sem.at[2 + part])))
    for when, copy in own:
        pl.when(when)(copy.start)

    zeros[...] = jnp.zeros_like(zeros)
    blank = []
    for when, columns in ((my_slab < 7, pl.ds(live, width - live)), (my_slab == 7, pl.ds(0, width))):
        blank.append((when, pltpu.make_async_copy(zeros.at[:, columns], got_unit.at[:, columns], local_sem.at[4])))
    for when, copy in blank:
        pl.when(when)(copy.start)
    acc[...] = jnp.zeros_like(acc)

    for when, copy in own:
        pl.when(when)(copy.wait)

    tile = min(256, upper)
    limits = []

    def accumulate(slab):
        @pl.when(slab < 7)
        def _():
            row = pl.multiple_of(slab * 2 * rows, rows)
            first_row = (slab // 2) * (4 * rows) + (slab % 2) * (2 * rows) + core * rows
            row_ids = first_row + lax.broadcasted_iota(jnp.int32, (rows, lower), 0)
            keep = (row_ids < limits[0]).astype(jnp.float32).astype(jnp.bfloat16)
            low_re = low[pl.ds(row, rows)] * keep
            low_im = low[pl.ds(pl.multiple_of(row + rows, rows), rows)] * keep
            swapped[0, :rows] = low_re
            swapped[0, rows:] = low_im
            swapped[1, :rows] = low_im
            swapped[1, rows:] = -low_re

            @pl.loop(0, upper // tile)
            def _(n):
                start = pl.multiple_of(n * tile, tile)
                left = up[pl.ds(row, 2 * rows), pl.ds(start, tile)]
                for part in range(2):
                    acc[part, pl.ds(start, tile)] += lax.dot_general(
                        left, swapped[part], (((0,), (0,)), ((), ())), preferred_element_type=jnp.float32)

    def wait_piece(at_y, kind, slab, part):
        if kind == UPPER:
            for size_when, count in ((x < 3, upper), (x == 3, 2 * rows)):
                here = piece(up, slab, part, count)
                pl.when((slab < 7) & size_when)(
                    remote(here, here, send_up.at[0], recv_up.at[slab, part], device(1, 0)).wait_recv)
        else:
            here = piece(low, slab, part, low_count(at_y))
            pl.when(slab < 7)(remote(here, here, send_low.at[0], recv_low.at[slab, part], device(1, 0)).wait_recv)

    def go_on(at_y, kind, dx, dhalf, part):
        if kind == LOWER:
            usual = part == (0 if dx == 3 else 1)
            if dx == 0:
                when = None
            elif usual:
                when = None if dhalf == 0 else (lambda: x != 1)
            else:
                when = (lambda: x == 3) if dhalf == 1 else (lambda: x < 0)
            count = low_count(at_y)
            for to_dx in ((1, 3) if dx == 0 else (4 - dx,)):
                send_low_piece(
                    at_y, lambda slab: piece(low, slab, part, count), part, dx, dhalf, (to_dx, 0), count, when)
            return
        when = None
        if at_y % 2 == 1:
            hops = [(part, 1 + 2 * part)]
        elif dhalf == 1:
            hops = [(part, 1 + 2 * part)]
            when = lambda: x < 3
        elif part == 0:
            hops = [(0, 1)]
        else:
            hops = [(1, 3), (0, 3), (1, 1)]
        for of_part, dy in hops:
            send_up_piece(
                at_y, when, lambda slab, count, of_part=of_part: piece(up, slab, of_part, count),
                of_part, dx, dhalf, (0, dy))

    def relay(at_y, part):
        dy = 1 + 2 * part
        count = low_count(at_y + dy)
        here = transit.at[pl.ds(part * rows, rows), pl.ds(0, count)]
        pl.when(slab_at(0, 1 - part) < 7)(
            remote(here, here, send_low.at[0], recv_transit.at[part], device(1, 0)).wait_recv)
        send_low_piece(at_y, lambda slab: here, part, 0, 1 - part, (0, dy), count)

    def steps(at_y):
        cut = [[]]
        for event in ORDER[at_y]:
            cut[-1].append(event)
            if event[0] == SUM:
                cut.append([])
        return cut

    waited = [{(UPPER if at_y % 2 == 0 else LOWER, 0, 0, part) for part in range(2)} for at_y in range(4)]

    def react(at_y, events):
        used.update(marks[at_y])
        for kind, *where in events:
            if kind == RELAY:
                relay(at_y, *where)
            elif kind == SUM:
                for piece_kind in (UPPER, LOWER):
                    for part in range(2):
                        key = (piece_kind, *where, part)
                        if key not in waited[at_y]:
                            wait_piece(at_y, piece_kind, slab_at(*where), part)
                        waited[at_y].add(key)
            else:
                wait_piece(at_y, kind, slab_at(*where[:2]), where[2])
                waited[at_y].add((kind, *where))
                go_on(at_y, kind, *where)
        marks[at_y] = dict(used)

    for n in range(8):
        slab = my_slab * 0
        for at_y in range(4):
            events = steps(at_y)[n]
            pl.when(y == at_y)(functools.partial(react, at_y, events))
            slab = jnp.where(y == at_y, slab_at(*events[-1][1:]), slab)
        if n == 0:
            meta_copy.wait()
            first = jnp.where(is_upper, mine[...], theirs[...])
            second = jnp.where(is_upper, theirs[...], mine[...])
            upper_count, lower_count = first[:, width:width + 1], second[:, width:width + 1]
            upper_deg = (2 * first[:, width + LANES:width + LANES + 1] + 1).astype(jnp.float32)
            lower_deg = (2 * second[:, width + LANES:width + LANES + 1] + 1).astype(jnp.float32)
            factor = 2.0 * lower_deg / (upper_deg + lower_deg)
            labels[0:1, :] = first
            labels[1:2, :] = second
            table = recoup[...] * allowed[...].astype(jnp.float32)
            levels = table.shape[0]
            c_start = pl.multiple_of(x * upper, LANES)
            d_start = pl.multiple_of(y * main, LANES)
            c_labels = labels[0:1, pl.ds(c_start, upper)]
            d_labels = labels[1:2, pl.ds(d_start, lower)]
            c_open = c_start + lax.broadcasted_iota(jnp.int32, (1, upper), 1) < upper_count
            d_open = d_start + lax.broadcasted_iota(jnp.int32, (1, lower), 1) < lower_count
            c_labels = jnp.where(c_open, c_labels, -1)
            d_labels = jnp.where(d_open, d_labels, -1)
            c_hot = (lax.broadcasted_iota(jnp.int32, (levels, upper), 0) == c_labels).astype(jnp.float32)
            d_hot = (lax.broadcasted_iota(jnp.int32, (levels, lower), 0) == d_labels).astype(jnp.float32)
            picked = factor * jnp.dot(
                table, d_hot, precision=lax.Precision.HIGHEST, preferred_element_type=jnp.float32)
            weight[...] = lax.dot_general(
                c_hot, picked, (((0,), (0,)), ((), ())),
                precision=lax.Precision.HIGHEST, preferred_element_type=jnp.float32)
            least = jnp.minimum(upper_count, lower_count)
            limits.append(least)
        accumulate(slab)

    order = (2, 1, 3, 0)

    def rows_of(to_y, of_core):
        return pl.ds(pl.multiple_of((to_y // 2) * (2 * rows) + of_core * rows, rows), rows)

    sums = []
    for n, dy in enumerate(order):
        to_y = (y + dy) % 4
        when = (x < 3) | (to_y < 2)
        copy = remote(
            acc.at[to_y % 2, rows_of(to_y, 1 - core)], other.at[n], send_sum.at[n], recv_sum.at[n], device(0, 0, 1))
        pl.when(when)(copy.start)
        sums.append((when, copy))

    def out_counts(of_y):
        return ((of_y < 3, main), (of_y == 3, lower))

    outs, kept = [], []
    for n, dy in enumerate(order):
        to_y = (y + dy) % 4
        when, copy = sums[n]

        @pl.when(when)
        def _(n=n, to_y=to_y, copy=copy):
            copy.wait_recv()
            keep = rows_of(to_y, core)
            value = weight[keep] * (acc[to_y % 2, keep] + other[n])
            largest = jnp.max(jnp.abs(value), axis=0, keepdims=True)
            over = jnp.where(largest > 0.0, 1.0 / largest, 0.0)
            coded[n] = jnp.round(value * over * 32767.0).astype(jnp.int32).astype(jnp.int16)
            unit[n] = largest

        for size_when, count in out_counts(y):
            here = when & size_when
            columns = pl.ds(d_start, count)
            pairs = (
                (unit.at[n, :, pl.ds(0, count)], got_unit.at[:, columns], 1),
                (coded.at[n, :, pl.ds(0, count)], got.at[:, columns], 0),
            )
            for src, dst, m in pairs:
                if dy == 0:
                    kept.append((here, pltpu.make_async_copy(src, dst, local_sem.at[5 + m])))
                    pl.when(here)(kept[-1][1].start)
                else:
                    outs.append((here, remote(src, dst, send_out.at[m, n], recv_out.at[m, y], device(0, dy))))
                    pl.when(here)(outs[-1][1].start)

    have_out = (x < 3) | (half == 0)
    for dy in (1, 3, 2):
        from_y = (y + dy) % 4
        for size_when, count in out_counts(from_y):
            @pl.when(have_out & size_when)
            def _(from_y=from_y, count=count):
                columns = pl.ds(pl.multiple_of(from_y * main, LANES), count)
                for m, here in ((1, got_unit.at[:, columns]), (0, got.at[:, columns])):
                    remote(here, here, send_out.at[m, 0], recv_out.at[m, from_y], device(1, 0)).wait_recv()

    for when, copy in blank + kept:
        pl.when(when)(copy.wait)
    for at_y in range(4):
        @pl.when(y == at_y)
        def _(at_y=at_y):
            for make in pending[at_y]:
                for when, copy in make():
                    pl.when(when)(copy.wait_send)
    for when, copy in sums + outs:
        pl.when(when)(copy.wait_send)


def per_device(s_real, s_imag, chan_l, counts, jlevel, allowed, recoup):
    rows, width = s_real.shape[1:]
    live, upper, main, extra, lower = plan(rows, width)
    vmem, anywhere = pl.BlockSpec(memory_space=pltpu.VMEM), pl.BlockSpec(memory_space=pl.ANY)
    dma = pltpu.SemaphoreType.DMA
    got, unit = pl.pallas_call(
        functools.partial(kernel, rows, width),
        grid=(1,),
        out_shape=(jax.ShapeDtypeStruct((rows, width), jnp.int16), jax.ShapeDtypeStruct((1, width), jnp.float32)),
        in_specs=[anywhere] * 3 + [vmem] * 2 + [anywhere] * 2,
        out_specs=(anywhere, anywhere),
        scratch_shapes=[
            pltpu.VMEM(chan_l.shape, jnp.int32),
            pltpu.VMEM(allowed.shape, jnp.int32),
            pltpu.VMEM(recoup.shape, jnp.float32),
            pltpu.VMEM((14 * rows, upper), jnp.bfloat16),
            pltpu.VMEM((14 * rows, lower), jnp.bfloat16),
            pltpu.VMEM((2 * rows, lower), jnp.bfloat16),
            pltpu.VMEM((2, 2 * rows, lower), jnp.bfloat16),
            pltpu.VMEM((2, upper, lower), jnp.float32),
            pltpu.VMEM((4, rows, lower), jnp.float32),
            pltpu.VMEM((4, rows, lower), jnp.int16),
            pltpu.VMEM((4, 1, lower), jnp.float32),
            pltpu.VMEM((upper, lower), jnp.float32),
            pltpu.VMEM((1, width), jnp.float32),
            pltpu.VMEM((1, width + 2 * LANES), jnp.int32),
            pltpu.VMEM((1, width + 2 * LANES), jnp.int32),
            pltpu.VMEM((8, width + 2 * LANES), jnp.int32),
            dma((40,)), dma((7, 2)), dma((40,)), dma((7, 2)), dma((2,)),
            dma((4,)), dma((4,)), dma((2, 4)), dma((2, 4)), dma((12,)),
        ],
        compiler_params=pltpu.CompilerParams(
            collective_id=0, has_side_effects=True, vmem_limit_bytes=61 << 20),
        cost_estimate=pl.CostEstimate(
            flops=16 * 7 * rows * upper * lower, bytes_accessed=8 * rows * width, transcendentals=0),
    )(s_real, s_imag, chan_l, counts[:, None], jlevel[:, None], allowed, recoup)
    share = jnp.maximum(got.astype(jnp.float32) * (1.0 / 32767.0), -1.0)
    return (share * unit)[None]


def solution(mesh):
    placed = (
        P("jpair", "row", None),
        P("jpair", "row", None),
        P("jpair", None),
        P("jpair"),
        P("jpair"),
        P(),
        P(),
    )
    return jax.shard_map(
        per_device, mesh=mesh, in_specs=placed, out_specs=P("jpair", "row", None), check_vma=False
    )
```

```python
import functools

import jax
import jax.numpy as jnp
from jax import lax
from jax.experimental import pallas as pl
from jax.experimental.pallas import tpu as pltpu
from jax.sharding import PartitionSpec as P

MESH = pl.DeviceIdType.MESH
LANES = 128
RELAY, UPPER, LOWER, SUM = range(4)
ORDER = (
    (
        (RELAY, 0), (RELAY, 1), (UPPER, 1, 0, 0), (UPPER, 3, 0, 0), (LOWER, 0, 1, 0), (LOWER, 0, 0, 0),
        (UPPER, 1, 0, 1), (LOWER, 0, 1, 1), (UPPER, 3, 0, 1), (LOWER, 0, 0, 1), (SUM, 0, 0), (LOWER, 1, 1, 0),
        (SUM, 0, 1), (UPPER, 2, 0, 0), (LOWER, 3, 1, 0), (LOWER, 1, 0, 0), (LOWER, 3, 0, 0), (UPPER, 2, 0, 1),
        (LOWER, 1, 1, 1), (LOWER, 3, 1, 1), (SUM, 1, 1), (LOWER, 1, 0, 1), (LOWER, 3, 0, 1), (SUM, 3, 1),
        (SUM, 1, 0), (SUM, 3, 0), (SUM, 2, 0), (SUM, 2, 1),
    ),
    (
        (LOWER, 1, 0, 0), (LOWER, 3, 0, 0), (UPPER, 0, 0, 0), (UPPER, 0, 1, 1), (LOWER, 1, 0, 1), (LOWER, 3, 0, 1),
        (LOWER, 0, 1, 0), (LOWER, 0, 1, 1), (UPPER, 1, 0, 0), (SUM, 0, 1), (LOWER, 3, 1, 0), (LOWER, 1, 1, 0),
        (UPPER, 1, 1, 1), (UPPER, 3, 0, 0), (LOWER, 3, 1, 1), (LOWER, 1, 1, 1), (SUM, 1, 1), (SUM, 1, 0),
        (UPPER, 3, 1, 1), (SUM, 3, 0), (UPPER, 2, 0, 0), (SUM, 3, 1), (UPPER, 2, 1, 1), (SUM, 0, 0), (SUM, 2, 0),
        (SUM, 2, 1),
    ),
    (
        (RELAY, 1), (RELAY, 0), (UPPER, 1, 0, 0), (UPPER, 3, 0, 0), (LOWER, 0, 0, 0), (LOWER, 0, 1, 0),
        (UPPER, 1, 0, 1), (UPPER, 3, 0, 1), (LOWER, 0, 0, 1), (LOWER, 0, 1, 1), (SUM, 0, 0), (UPPER, 0, 1, 1),
        (UPPER, 0, 1, 0), (LOWER, 1, 0, 0), (SUM, 0, 1), (UPPER, 2, 0, 0), (LOWER, 1, 1, 0), (LOWER, 3, 0, 0),
        (LOWER, 1, 0, 1), (LOWER, 3, 1, 0), (SUM, 1, 0), (UPPER, 2, 0, 1), (LOWER, 1, 1, 1), (LOWER, 3, 0, 1),
        (SUM, 1, 1), (SUM, 3, 0), (LOWER, 3, 1, 1), (SUM, 3, 1), (SUM, 2, 0), (SUM, 2, 1),
    ),
    (
        (UPPER, 0, 0, 0), (UPPER, 0, 1, 1), (LOWER, 1, 0, 0), (LOWER, 3, 0, 0), (LOWER, 1, 0, 1), (LOWER, 3, 0, 1),
        (LOWER, 0, 1, 1), (SUM, 0, 0), (LOWER, 0, 1, 0), (UPPER, 1, 1, 1), (UPPER, 1, 0, 0), (LOWER, 3, 1, 1),
        (LOWER, 1, 1, 1), (UPPER, 3, 0, 0), (LOWER, 3, 1, 0), (UPPER, 3, 1, 1), (LOWER, 1, 1, 0), (SUM, 1, 1),
        (SUM, 1, 0), (SUM, 3, 1), (UPPER, 2, 0, 0), (UPPER, 2, 1, 1), (SUM, 3, 0), (SUM, 0, 1), (SUM, 2, 0),
        (SUM, 2, 1),
    ),
)


def plan(rows, width):
    live = 14 * rows
    upper = 4 * rows
    main = live // LANES // 4 * LANES
    extra = live - 4 * main
    return live, upper, main, extra, main + extra


def kernel(
    rows, width, re_ref, im_ref, chan_ref, count_ref, level_ref, allowed_ref, recoup_ref, got, got_unit,
    chan, allowed, recoup,
    up, low, transit, swapped, acc, other, coded, unit, weight, zeros, mine, theirs, labels,
    send_up, recv_up, send_low, recv_low, recv_transit, send_sum, recv_sum, send_out, recv_out, local_sem,
):
    live, upper, main, extra, lower = plan(rows, width)
    j, r = lax.axis_index("jpair"), lax.axis_index("row")
    pair, parity = j // 2, j % 2
    x, half, core = r // 4, (r // 2) % 2, r % 2
    y = 2 * half + parity
    is_upper, is_lower = parity == 0, parity == 1
    source = (re_ref, im_ref)

    def device(dx, dy, dcore=0):
        to_x, to_y = (x + dx) % 4, (y + dy) % 4
        return (2 * pair + to_y % 2, 4 * to_x + 2 * (to_y // 2) + (core + dcore) % 2)

    def remote(src, dst, send, recv, where):
        return pltpu.make_async_remote_copy(
            src_ref=src, dst_ref=dst, send_sem=send, recv_sem=recv, device_id=where, device_id_type=MESH
        )

    small = [
        pltpu.make_async_copy(src, dst, local_sem.at[8 + n])
        for n, (src, dst) in enumerate(((chan_ref, chan), (allowed_ref, allowed), (recoup_ref, recoup)))]
    for copy in small:
        copy.start()
    barrier = pltpu.get_barrier_semaphore()
    greeted = [(1, 0, 0), (3, 0, 0), (2, 0, 0), (0, 1, 0), (0, 3, 0), (0, 2, 0), (0, 0, 1)]
    for offset in greeted:
        pl.semaphore_signal(barrier, inc=1, device_id=device(*offset), device_id_type=MESH)
    pl.semaphore_wait(barrier, len(greeted))

    def slab_at(dx, dhalf):
        return 2 * ((x + dx) % 4) + (half + dhalf) % 2

    def piece(buffer, slab, part, count):
        return buffer.at[pl.ds(pl.multiple_of(slab * (2 * rows) + part * rows, rows), rows), pl.ds(0, count)]

    my_slab = slab_at(0, 0)
    have_rows = my_slab < 7
    up_from, low_from = is_upper & have_rows, is_lower & have_rows

    for copy in small:
        copy.wait()
    mine[:, :width] = chan[...]
    mine[:, width:width + LANES] = jnp.broadcast_to(count_ref[...], (1, LANES))
    mine[:, width + LANES:] = jnp.broadcast_to(level_ref[...], (1, LANES))
    meta_copy = remote(mine, theirs, local_sem.at[0], local_sem.at[1], device(0, 1 - 2 * parity))
    meta_copy.start()

    def low_count(to_y):
        return lower if to_y % 4 == 3 else main

    def up_columns(part, to_x):
        return lambda count: source[part].at[0, :, pl.ds(pl.multiple_of(to_x * upper, LANES), count)]

    def low_columns(part, to_y, count):
        return source[part].at[0, :, pl.ds(pl.multiple_of(to_y * main, LANES), count)]

    pending = [[] for _ in range(4)]
    used = {"up": 0, "low": 0}

    def send(at_y, make):
        for when, copy in make():
            pl.when(when)(copy.start)
        pending[at_y].append(make)

    def send_up_piece(at_y, when, src, part, dx, dhalf, to):
        n = used["up"]
        used["up"] += 1

        def make():
            slab = slab_at(dx, dhalf)
            ok = (slab < 7) if when is None else (slab < 7) & when()
            to_x = (x + to[0]) % 4
            return [
                (ok & size_when, remote(
                    src(slab, count), piece(up, slab, part, count), send_up.at[n], recv_up.at[slab, part], device(*to)))
                for size_when, count in ((to_x < 3, upper), (to_x == 3, 2 * rows))]

        send(at_y, make)

    def send_low_piece(at_y, src, part, dx, dhalf, to, count, when=None, passing=False):
        n = used["low"]
        used["low"] += 1

        def make():
            slab = slab_at(dx, dhalf)
            if passing:
                dst, recv = transit.at[pl.ds(part * rows, rows), pl.ds(0, count)], recv_transit.at[part]
            else:
                dst, recv = piece(low, slab, part, count), recv_low.at[slab, part]
            ok = (slab < 7) if when is None else (slab < 7) & when()
            return [(ok, remote(src(slab), dst, send_low.at[n], recv, device(*to)))]

        send(at_y, make)

    def begin(at_y):
        used["up"] = used["low"] = 0
        if at_y % 2 == 0:
            for part, dy in ((0, 1), (1, 3), (0, 3), (1, 1)):
                when = (lambda: x == 3) if at_y == 0 and dy != 1 + 2 * part else None
                send_up_piece(at_y, when, lambda slab, count, part=part: up_columns(part, x)(count), part, 0, 0, (0, dy))
            for dx in (1, 3, 2):
                for part in range(2):
                    send_up_piece(
                        at_y, None, lambda slab, count, part=part, dx=dx: up_columns(part, (x + dx) % 4)(count),
                        part, 0, 0, (dx, 0))
        else:
            to = [(0, part, 1 + 2 * part, at_y + 2) for part in range(2)]
            to += [(0, part, dy, at_y + dy) for part in range(2) for dy in (1, 3)]
            to += [(dx, part, 0, at_y) for part in range(2) for dx in (1, 3)]
            for n, (dx, part, dy, to_y) in enumerate(to):
                count = low_count(to_y)
                send_low_piece(
                    at_y, lambda slab, part=part, to_y=to_y, count=count: low_columns(part, to_y % 4, count),
                    part, 0, 0, (dx, dy), count, passing=n < 2)
        marks.append(dict(used))

    marks = []
    for at_y in range(4):
        pl.when(y == at_y)(functools.partial(begin, at_y))

    own = []
    for part in range(2):
        own.append((up_from, pltpu.make_async_copy(
            up_columns(part, x)(upper), piece(up, my_slab, part, upper), local_sem.at[2 + part])))
        own.append((low_from, pltpu.make_async_copy(
            low_columns(part, y, lower), piece(low, my_slab, part, lower), local_sem.at[2 + part])))
    for when, copy in own:
        pl.when(when)(copy.start)

    zeros[...] = jnp.zeros_like(zeros)
    blank = []
    for when, columns in ((my_slab < 7, pl.ds(live, width - live)), (my_slab == 7, pl.ds(0, width))):
        blank.append((when, pltpu.make_async_copy(zeros.at[:, columns], got_unit.at[:, columns], local_sem.at[4])))
    for when, copy in blank:
        pl.when(when)(copy.start)
    acc[...] = jnp.zeros_like(acc)

    for when, copy in own:
        pl.when(when)(copy.wait)

    tile = min(256, upper)
    limits = []

    def accumulate(slab):
        @pl.when(slab < 7)
        def _():
            row = pl.multiple_of(slab * 2 * rows, rows)
            first_row = (slab // 2) * (4 * rows) + (slab % 2) * (2 * rows) + core * rows
            row_ids = first_row + lax.broadcasted_iota(jnp.int32, (rows, lower), 0)
            keep = (row_ids < limits[0]).astype(jnp.float32).astype(jnp.bfloat16)
            low_re = low[pl.ds(row, rows)] * keep
            low_im = low[pl.ds(pl.multiple_of(row + rows, rows), rows)] * keep
            swapped[0, :rows] = low_re
            swapped[0, rows:] = low_im
            swapped[1, :rows] = low_im
            swapped[1, rows:] = -low_re

            @pl.loop(0, upper // tile)
            def _(n):
                start = pl.multiple_of(n * tile, tile)
                left = up[pl.ds(row, 2 * rows), pl.ds(start, tile)]
                for part in range(2):
                    acc[part, pl.ds(start, tile)] += lax.dot_general(
                        left, swapped[part], (((0,), (0,)), ((), ())), preferred_element_type=jnp.float32)

    def wait_piece(at_y, kind, slab, part):
        if kind == UPPER:
            for size_when, count in ((x < 3, upper), (x == 3, 2 * rows)):
                here = piece(up, slab, part, count)
                pl.when((slab < 7) & size_when)(
                    remote(here, here, send_up.at[0], recv_up.at[slab, part], device(1, 0)).wait_recv)
        else:
            here = piece(low, slab, part, low_count(at_y))
            pl.when(slab < 7)(remote(here, here, send_low.at[0], recv_low.at[slab, part], device(1, 0)).wait_recv)

    def go_on(at_y, kind, dx, dhalf, part):
        if kind == LOWER:
            usual = part == (0 if dx == 3 else 1)
            if dx == 0:
                when = None
            elif usual:
                when = None if dhalf == 0 else (lambda: x != 1)
            else:
                when = (lambda: x == 3) if dhalf == 1 else (lambda: x < 0)
            count = low_count(at_y)
            for to_dx in ((1, 3) if dx == 0 else (4 - dx,)):
                send_low_piece(
                    at_y, lambda slab: piece(low, slab, part, count), part, dx, dhalf, (to_dx, 0), count, when)
            return
        when = None
        if at_y % 2 == 1:
            hops = [(part, 1 + 2 * part)]
        elif dhalf == 1:
            hops = [(part, 1 + 2 * part)]
            when = lambda: x < 3
        elif part == 0:
            hops = [(0, 1)]
        else:
            hops = [(1, 3), (0, 3), (1, 1)]
        for of_part, dy in hops:
            send_up_piece(
                at_y, when, lambda slab, count, of_part=of_part: piece(up, slab, of_part, count),
                of_part, dx, dhalf, (0, dy))

    def relay(at_y, part):
        dy = 1 + 2 * part
        count = low_count(at_y + dy)
        here = transit.at[pl.ds(part * rows, rows), pl.ds(0, count)]
        pl.when(slab_at(0, 1 - part) < 7)(
            remote(here, here, send_low.at[0], recv_transit.at[part], device(1, 0)).wait_recv)
        send_low_piece(at_y, lambda slab: here, part, 0, 1 - part, (0, dy), count)

    def steps(at_y):
        cut = [[]]
        for event in ORDER[at_y]:
            cut[-1].append(event)
            if event[0] == SUM:
                cut.append([])
        return cut

    waited = [{(UPPER if at_y % 2 == 0 else LOWER, 0, 0, part) for part in range(2)} for at_y in range(4)]

    def react(at_y, events):
        used.update(marks[at_y])
        for kind, *where in events:
            if kind == RELAY:
                relay(at_y, *where)
            elif kind == SUM:
                for piece_kind in (UPPER, LOWER):
                    for part in range(2):
                        key = (piece_kind, *where, part)
                        if key not in waited[at_y]:
                            wait_piece(at_y, piece_kind, slab_at(*where), part)
                        waited[at_y].add(key)
            else:
                wait_piece(at_y, kind, slab_at(*where[:2]), where[2])
                waited[at_y].add((kind, *where))
                go_on(at_y, kind, *where)
        marks[at_y] = dict(used)

    for n in range(8):
        slab = my_slab * 0
        for at_y in range(4):
            events = steps(at_y)[n]
            pl.when(y == at_y)(functools.partial(react, at_y, events))
            slab = jnp.where(y == at_y, slab_at(*events[-1][1:]), slab)
        if n == 0:
            meta_copy.wait()
            first = jnp.where(is_upper, mine[...], theirs[...])
            second = jnp.where(is_upper, theirs[...], mine[...])
            upper_count, lower_count = first[:, width:width + 1], second[:, width:width + 1]
            upper_deg = (2 * first[:, width + LANES:width + LANES + 1] + 1).astype(jnp.float32)
            lower_deg = (2 * second[:, width + LANES:width + LANES + 1] + 1).astype(jnp.float32)
            factor = 2.0 * lower_deg / (upper_deg + lower_deg)
            labels[0:1, :] = first
            labels[1:2, :] = second
            table = recoup[...] * allowed[...].astype(jnp.float32)
            levels = table.shape[0]
            c_start = pl.multiple_of(x * upper, LANES)
            d_start = pl.multiple_of(y * main, LANES)
            c_labels = labels[0:1, pl.ds(c_start, upper)]
            d_labels = labels[1:2, pl.ds(d_start, lower)]
            c_open = c_start + lax.broadcasted_iota(jnp.int32, (1, upper), 1) < upper_count
            d_open = d_start + lax.broadcasted_iota(jnp.int32, (1, lower), 1) < lower_count
            c_labels = jnp.where(c_open, c_labels, -1)
            d_labels = jnp.where(d_open, d_labels, -1)
            c_hot = (lax.broadcasted_iota(jnp.int32, (levels, upper), 0) == c_labels).astype(jnp.float32)
            d_hot = (lax.broadcasted_iota(jnp.int32, (levels, lower), 0) == d_labels).astype(jnp.float32)
            picked = factor * jnp.dot(
                table, d_hot, precision=lax.Precision.HIGHEST, preferred_element_type=jnp.float32)
            weight[...] = lax.dot_general(
                c_hot, picked, (((0,), (0,)), ((), ())),
                precision=lax.Precision.HIGHEST, preferred_element_type=jnp.float32)
            least = jnp.minimum(upper_count, lower_count)
            limits.append(least)
        accumulate(slab)

    order = (2, 3 - 2 * parity, 1 + 2 * parity, 0)

    def rows_of(to_y, of_core):
        return pl.ds(pl.multiple_of((to_y // 2) * (2 * rows) + of_core * rows, rows), rows)

    sums = []
    for n, dy in enumerate(order):
        to_y = (y + dy) % 4
        when = (x < 3) | (to_y < 2)
        copy = remote(
            acc.at[to_y % 2, rows_of(to_y, 1 - core)], other.at[n], send_sum.at[n], recv_sum.at[n], device(0, 0, 1))
        pl.when(when)(copy.start)
        sums.append((when, copy))

    def out_counts(of_y):
        return ((of_y < 3, main), (of_y == 3, lower))

    outs, kept = [], []
    for n, dy in enumerate(order):
        to_y = (y + dy) % 4
        when, copy = sums[n]

        @pl.when(when)
        def _(n=n, to_y=to_y, copy=copy):
            copy.wait_recv()
            keep = rows_of(to_y, core)
            value = weight[keep] * (acc[to_y % 2, keep] + other[n])
            largest = jnp.max(jnp.abs(value), axis=0, keepdims=True)
            over = jnp.where(largest > 0.0, 1.0 / largest, 0.0)
            coded[n] = jnp.round(value * over * 32767.0).astype(jnp.int32).astype(jnp.int16)
            unit[n] = largest

        for size_when, count in out_counts(y):
            here = when & size_when
            columns = pl.ds(d_start, count)
            pairs = (
                (unit.at[n, :, pl.ds(0, count)], got_unit.at[:, columns], 1),
                (coded.at[n, :, pl.ds(0, count)], got.at[:, columns], 0),
            )
            for src, dst, m in pairs:
                if n == 3:
                    kept.append((here, pltpu.make_async_copy(src, dst, local_sem.at[5 + m])))
                    pl.when(here)(kept[-1][1].start)
                else:
                    outs.append((here, remote(src, dst, send_out.at[m, n], recv_out.at[m, y], device(0, dy))))
                    pl.when(here)(outs[-1][1].start)

    have_out = (x < 3) | (half == 0)
    for dy in (1, 3, 2):
        from_y = (y + dy) % 4
        for size_when, count in out_counts(from_y):
            @pl.when(have_out & size_when)
            def _(from_y=from_y, count=count):
                columns = pl.ds(pl.multiple_of(from_y * main, LANES), count)
                for m, here in ((1, got_unit.at[:, columns]), (0, got.at[:, columns])):
                    remote(here, here, send_out.at[m, 0], recv_out.at[m, from_y], device(1, 0)).wait_recv()

    for when, copy in blank + kept:
        pl.when(when)(copy.wait)
    for at_y in range(4):
        @pl.when(y == at_y)
        def _(at_y=at_y):
            for make in pending[at_y]:
                for when, copy in make():
                    pl.when(when)(copy.wait_send)
    for when, copy in sums + outs:
        pl.when(when)(copy.wait_send)


def per_device(s_real, s_imag, chan_l, counts, jlevel, allowed, recoup):
    rows, width = s_real.shape[1:]
    live, upper, main, extra, lower = plan(rows, width)
    vmem, anywhere = pl.BlockSpec(memory_space=pltpu.VMEM), pl.BlockSpec(memory_space=pl.ANY)
    dma = pltpu.SemaphoreType.DMA
    got, unit = pl.pallas_call(
        functools.partial(kernel, rows, width),
        grid=(1,),
        out_shape=(jax.ShapeDtypeStruct((rows, width), jnp.int16), jax.ShapeDtypeStruct((1, width), jnp.float32)),
        in_specs=[anywhere] * 3 + [vmem] * 2 + [anywhere] * 2,
        out_specs=(anywhere, anywhere),
        scratch_shapes=[
            pltpu.VMEM(chan_l.shape, jnp.int32),
            pltpu.VMEM(allowed.shape, jnp.int32),
            pltpu.VMEM(recoup.shape, jnp.float32),
            pltpu.VMEM((14 * rows, upper), jnp.bfloat16),
            pltpu.VMEM((14 * rows, lower), jnp.bfloat16),
            pltpu.VMEM((2 * rows, lower), jnp.bfloat16),
            pltpu.VMEM((2, 2 * rows, lower), jnp.bfloat16),
            pltpu.VMEM((2, upper, lower), jnp.float32),
            pltpu.VMEM((4, rows, lower), jnp.float32),
            pltpu.VMEM((4, rows, lower), jnp.int16),
            pltpu.VMEM((4, 1, lower), jnp.float32),
            pltpu.VMEM((upper, lower), jnp.float32),
            pltpu.VMEM((1, width), jnp.float32),
            pltpu.VMEM((1, width + 2 * LANES), jnp.int32),
            pltpu.VMEM((1, width + 2 * LANES), jnp.int32),
            pltpu.VMEM((8, width + 2 * LANES), jnp.int32),
            dma((40,)), dma((7, 2)), dma((40,)), dma((7, 2)), dma((2,)),
            dma((4,)), dma((4,)), dma((2, 4)), dma((2, 4)), dma((12,)),
        ],
        compiler_params=pltpu.CompilerParams(
            collective_id=0, has_side_effects=True, vmem_limit_bytes=61 << 20),
        cost_estimate=pl.CostEstimate(
            flops=16 * 7 * rows * upper * lower, bytes_accessed=8 * rows * width, transcendentals=0),
    )(s_real, s_imag, chan_l, counts[:, None], jlevel[:, None], allowed, recoup)
    share = jnp.maximum(got.astype(jnp.float32) * (1.0 / 32767.0), -1.0)
    return (share * unit)[None]


def solution(mesh):
    placed = (
        P("jpair", "row", None),
        P("jpair", "row", None),
        P("jpair", None),
        P("jpair"),
        P("jpair"),
        P(),
        P(),
    )
    return jax.shard_map(
        per_device, mesh=mesh, in_specs=placed, out_specs=P("jpair", "row", None), check_vma=False
    )
```
